32 devices in a mesh: ctx: 2 (over x), head: 4 (over y, core), rep: 4 (over z).
Axes of the slice: x: 2, y: 2, z: 4, core: 2. Of those that a mesh axis runs over, the one named last changes fastest.
Arguments:
- kv_cache: float32 [8, 2, 512, 8, 128], P('head', None, 'ctx', 'rep'), may hold values from -8 to 8
- prefill_q: float32 [8, 256, 64, 128], P('head', 'ctx', 'rep'), may hold values from -512 to 512
- decode_q: float32 [8, 8, 4, 64, 128], P(None, ('ctx', 'rep'), None, 'head'), may hold values from -512 to 512
- decode_kv: float32 [8, 8, 4, 2, 8, 128], P(None, ('ctx', 'rep'), None, None, 'head'), may hold values from -12 to 12
- lengths: int32 [8], replicated, may hold values from 256 to 512, as said below
- row_length: int32 [8, 8], P(None, ('ctx', 'rep')), may hold values from 2 to 512, as said below
Outputs:
- prefill_out: float32 [8, 256, 64, 128], P('head', 'ctx', 'rep')
- decode_out: float32 [8, 8, 4, 64, 128], P(None, ('ctx', 'rep'), None, 'head')
The draws below stay inside these ranges and needn't reach their ends.
Inputs may be any that keep to these rules, and one draw needn't show every extreme that they name: `lengths`: multiples of 128; some request has length 512. `row_length`: a row reads at most its request's length; every request has a row that reads its whole length.
All inputs are finite; a program needn't handle non-finite values.
Results may differ from the reference program's by a relative error of at most 0.0003.
Values sent between devices are 32-bit elements; how exact they have to be, the bound alone decides.
No kernel may reach another device: no remote copies, remote signals or barrier semaphores. Data moves between devices by JAX's collectives and lax.ppermute only.
A program may use at most 128 MiB of HBM per device.

```python
import math
import jax
import jax.numpy as jnp
from jax import lax

HD = 128
KVH = 8
QH = 64
REQS = 8
LMAX = 512
GRAIN = 128
SPAN = 256
STEPS = 4
ROWS_REQ = 8


def length_table(key):
    base_key = jax.random.fold_in(key, 7)
    lowest = max(SPAN, LMAX // 4 // GRAIN * GRAIN) // GRAIN
    unit_counts = jax.random.randint(jax.random.fold_in(base_key, 1), (REQS,), lowest, LMAX // GRAIN + 1)
    longest = jax.random.randint(jax.random.fold_in(base_key, 2), (), 0, REQS)
    unit_counts = jnp.where(jnp.arange(REQS) == longest, LMAX // GRAIN, unit_counts)
    return (unit_counts * GRAIN).astype(jnp.int32)


def draw_lengths(key, part):
    return length_table(key)


def draw_row_length(key, part):
    totals = length_table(key)
    base_key = jax.random.fold_in(key, 8)
    raw_bits = jax.random.randint(jax.random.fold_in(base_key, 1), (REQS, ROWS_REQ), 0, 1 << 30)
    drawn = 2 + raw_bits % (totals[:, None] - 1)
    full_row = jax.random.randint(jax.random.fold_in(base_key, 2), (REQS,), 0, ROWS_REQ)
    drawn = jnp.where(jnp.arange(ROWS_REQ)[None, :] == full_row[:, None], totals[:, None], drawn)
    return drawn.astype(jnp.int32)


def draw_kv_cache(key, part):
    own_key = jax.random.fold_in(key, 21)
    drawn_shape = (REQS, 2, LMAX, KVH, HD)
    drawn = jnp.clip(jax.random.normal(own_key, drawn_shape), -6.0, 6.0)
    return drawn.astype(jnp.float32)


def draw_prefill_q(key, part):
    own_key = jax.random.fold_in(key, 31)
    drawn_shape = (REQS, SPAN, QH, HD)
    drawn = 2.5 * jnp.clip(jax.random.normal(own_key, drawn_shape), -6.0, 6.0)
    return jnp.clip(drawn, -500.0, 500.0).astype(jnp.float32)


def draw_decode_q(key, part):
    own_key = jax.random.fold_in(key, 41)
    drawn_shape = (REQS, ROWS_REQ, STEPS, QH, HD)
    drawn = 2.5 * jnp.clip(jax.random.normal(own_key, drawn_shape), -6.0, 6.0)
    return jnp.clip(drawn, -500.0, 500.0).astype(jnp.float32)


def block_levels(key, shape, split, smallest, largest):
    def one(axis_at, shards_of):
        draws = jax.random.uniform(jax.random.fold_in(jax.random.fold_in(key, 6), axis_at), (shards_of,), jnp.float32, smallest / len(split), largest / len(split))
        return jnp.repeat(jnp.exp(draws), shape[axis_at] // shards_of).reshape((-1,) + (1,) * (len(shape) - axis_at - 1))

    loudness = one(*split[0])
    for cut in split[1:]:
        loudness = loudness * one(*cut)
    return loudness


def normal_values(stream_key, extent, deviation, most, cuts=(), kind=jnp.bfloat16):
    entries = deviation * jax.random.normal(stream_key, extent, jnp.float32)
    if cuts:
        entries = entries * block_levels(stream_key, extent, cuts, -0.22, 0.18)
    return jnp.clip(entries, -most, most).astype(kind)


def setup_inputs(seed: int = 0) -> dict:
    splits = jax.random.split(jax.random.key(seed), 7)
    kv_cache = draw_kv_cache(jax.random.fold_in(splits[6], 71), 0)
    prefill_q = draw_prefill_q(jax.random.fold_in(splits[6], 71), 0)
    decode_q = draw_decode_q(jax.random.fold_in(splits[6], 71), 0)
    decode_kv = normal_values(splits[3], (REQS, ROWS_REQ, STEPS, 2, KVH, HD), 2.0, 12.0, ((1, 8), (4, 4)), jnp.float32)
    lengths = draw_lengths(jax.random.fold_in(splits[6], 71), 0)
    row_length = draw_row_length(jax.random.fold_in(splits[6], 71), 0)
    return {"kv_cache": kv_cache, "prefill_q": prefill_q, "decode_q": decode_q, "decode_kv": decode_kv, "lengths": lengths, "row_length": row_length}


NEG_FILL = -1e+30
HIGH_PRECISION = lax.Precision.HIGHEST

def prefill_one(inputs):
    queries, cache_rows, length = inputs
    score_scale = 1.0 / math.sqrt(HD)
    grouped = queries.reshape(SPAN, KVH, QH // KVH, HD)
    scores = jnp.einsum('qkgd,pkd->kgqp', grouped, cache_rows[0], precision=HIGH_PRECISION) * score_scale
    query_pos = length - SPAN + jnp.arange(SPAN, dtype=jnp.int32)
    allowed = jnp.arange(LMAX, dtype=jnp.int32)[None, :] <= query_pos[:, None]
    scores = jnp.where(allowed[None, None], scores, NEG_FILL)
    weights = jax.nn.softmax(scores, axis=-1)
    blended = jnp.einsum('kgqp,pkd->qkgd', weights, cache_rows[1], precision=HIGH_PRECISION)
    return blended.reshape(SPAN, QH, HD)

def decode_one(inputs):
    queries, drafts, cache_rows, limits = inputs
    score_scale = 1.0 / math.sqrt(HD)
    grouped = queries.reshape(ROWS_REQ, STEPS, KVH, QH // KVH, HD)
    context = jnp.einsum('rtkgd,pkd->rtkgp', grouped, cache_rows[0], precision=HIGH_PRECISION) * score_scale
    visible = jnp.arange(LMAX, dtype=jnp.int32)[None, :] < limits[:, None]
    context = jnp.where(visible[:, None, None, None, :], context, NEG_FILL)
    own_scores = jnp.einsum('rtkgd,rskd->rtkgs', grouped, drafts[:, :, 0], precision=HIGH_PRECISION) * score_scale
    step_ids = jnp.arange(STEPS, dtype=jnp.int32)
    causal = step_ids[None, :] <= step_ids[:, None]
    own_scores = jnp.where(causal[None, :, None, None, :], own_scores, NEG_FILL)
    weights = jax.nn.softmax(jnp.concatenate([context, own_scores], axis=-1), axis=-1)
    blended = jnp.einsum('rtkgp,pkd->rtkgd', weights[..., :LMAX], cache_rows[1], precision=HIGH_PRECISION)
    blended = blended + jnp.einsum('rtkgs,rskd->rtkgd', weights[..., LMAX:], drafts[:, :, 1], precision=HIGH_PRECISION)
    return blended.reshape(ROWS_REQ, STEPS, QH, HD)

def reference(kv_cache, prefill_q, decode_q, decode_kv, lengths, row_length):
    prefill_out = lax.map(prefill_one, (prefill_q, kv_cache, lengths))
    decode_out = lax.map(decode_one, (decode_q, decode_kv, kv_cache, row_length))
    return (prefill_out, decode_out)
```

```python
import functools
import math

import jax
import jax.numpy as jnp
from jax import lax
from jax.experimental import pallas as pl
from jax.experimental.pallas import tpu as pltpu
from jax.sharding import PartitionSpec as P

NEG_FILL = -1e30
LOG2E = math.log2(math.e)
F32 = jnp.float32
BF16 = jnp.bfloat16


def split_two(x):
    high = x.astype(BF16)
    return high, (x - high.astype(F32)).astype(BF16)


def split_three(x):
    high = x.astype(BF16)
    rest = x - high.astype(F32)
    mid = rest.astype(BF16)
    return high, mid, (rest - mid.astype(F32)).astype(BF16)


def query_terms(q):
    a, b, c = split_three(q)
    return jnp.concatenate([a, b, a, b, a, c], axis=-1)


def key_terms(k):
    a, b, c = split_three(k)
    return jnp.concatenate([a, a, b, b, c, a], axis=-1)


def value_terms(v):
    return jnp.concatenate(split_two(v), axis=-1)


def scores_of(q6, k6):
    return lax.dot_general(q6, k6, (((1,), (1,)), ((), ())), preferred_element_type=F32)


def weighted(p, vv):
    half = vv.shape[1] // 2
    a, b = split_two(p)
    both = jnp.dot(a, vv, preferred_element_type=F32) + jnp.dot(b, vv, preferred_element_type=F32)
    return both[:, :half] + both[:, half:]


def attend(q6, groups):
    state = None
    for group in groups:
        parts = [jnp.where(mask(), scores_of(q6, k6), NEG_FILL) for k6, _, mask in group]
        top = functools.reduce(jnp.maximum, [jnp.max(s, axis=-1, keepdims=True) for s in parts])
        if state is not None:
            top = jnp.maximum(top, state[0])
        weights = [jnp.exp2(s - top) for s in parts]
        total = functools.reduce(jnp.add, [jnp.sum(w, axis=-1, keepdims=True) for w in weights])
        acc = functools.reduce(jnp.add, [weighted(w, vv) for w, (_, vv, _) in zip(weights, group)])
        if state is not None:
            factor = jnp.exp2(state[0] - top)
            total = total + state[1] * factor
            acc = acc + state[2] * factor
        state = (top, total, acc)
    return state[2] / state[1]


def in_pairs(blocks):
    return [blocks[i : i + 2] for i in range(0, len(blocks), 2)]


def cache_head(ref, which, head, heads):
    rows = ref.shape[2] // heads
    return ref[0, which, pl.ds(head, rows, stride=heads), :]


def prefill_kernel(blocks, heads, group, scale, marks, q_ref, *refs):
    kv_refs, o_ref = refs[:blocks], refs[-1]
    span = q_ref.shape[1]
    dim = q_ref.shape[3]
    head = pl.program_id(0)
    keys = [key_terms(cache_head(ref, 0, head, heads)) for ref in kv_refs]
    vals = [value_terms(cache_head(ref, 1, head, heads)) for ref in kv_refs]
    chunk = min(span, 64)
    for first in range(0, span, chunk):
        q = q_ref[0, first : first + chunk].reshape(chunk * group, dim) * scale
        q6 = query_terms(q)

        def mask_of(b, first=first):
            shape = (chunk * group, keys[b].shape[0])
            pos = marks[1 + b] + lax.broadcasted_iota(jnp.int32, shape, 1)
            row = lax.broadcasted_iota(jnp.int32, shape, 0) // group
            return pos <= row + (marks[0] + first)

        todo = [(keys[b], vals[b], functools.partial(mask_of, b)) for b in range(blocks)]
        out = attend(q6, in_pairs(todo))
        o_ref[0, first : first + chunk] = out.reshape(chunk, group, dim)


def prefill_request(index, marks, prefill_q, kv_list, carried, heads, scale):
    nreq, span, q_heads, dim = prefill_q.shape
    group = q_heads // heads
    blocks = len(kv_list)
    q_spec = pl.BlockSpec((1, span, group, dim), lambda k, m: (index, 0, k, 0))
    kv_specs = [pl.BlockSpec(kv.shape, lambda k, m: (0, 0, 0, 0)) for kv in kv_list]
    extra_specs, extra, alias = [], [], {}
    if carried is not None:
        extra_specs, extra = [pl.BlockSpec(memory_space=pl.ANY)], [carried]
        alias = {2 + blocks: 0}
    keys = sum(kv.shape[2] for kv in kv_list)
    return pl.pallas_call(
        functools.partial(prefill_kernel, blocks, heads, group, scale),
        grid_spec=pltpu.PrefetchScalarGridSpec(
            num_scalar_prefetch=1,
            grid=(heads,),
            in_specs=[q_spec] + kv_specs + extra_specs,
            out_specs=q_spec,
        ),
        out_shape=jax.ShapeDtypeStruct(prefill_q.shape, F32),
        input_output_aliases=alias,
        compiler_params=pltpu.CompilerParams(vmem_limit_bytes=40 * 2**20),
        cost_estimate=pl.CostEstimate(
            flops=2 * 10 * span * group * keys * dim,
            bytes_accessed=4 * (2 * span * q_heads * dim + 2 * keys * dim),
            transcendentals=span * group * keys,
        ),
        name="prefill",
    )(marks, prefill_q, *kv_list, *extra)


def decode_kernel(blocks, packets, heads, group, steps, scale, marks, *refs):
    pk_refs = refs[:packets]
    kv_refs = refs[packets : packets + blocks]
    out_refs = refs[-packets:]
    per = pk_refs[0].shape[1]
    dim = pk_refs[0].shape[3]
    q_rows = steps * heads * group
    rows = steps * group
    slots = [(ref, n) for ref in pk_refs for n in range(per)]
    limit = jnp.concatenate(
        [
            jnp.broadcast_to(ref[0, n, q_rows + 4 * steps : q_rows + 4 * steps + 1, 0:1], (rows, 1))
            for ref, n in slots
        ],
        axis=0,
    ).astype(jnp.int32)
    for head in range(heads):
        q = jnp.concatenate(
            [
                ref[0, n, 0:q_rows].reshape(steps, heads * group, dim)[:, head * group : (head + 1) * group].reshape(rows, dim)
                for ref, n in slots
            ],
            axis=0,
        )
        q6 = query_terms(q * scale)
        todo = []
        for b, ref in enumerate(kv_refs):
            k6 = key_terms(cache_head(ref, 0, head, heads))
            vv = value_terms(cache_head(ref, 1, head, heads))

            def visible(b=b, count=k6.shape[0]):
                pos = marks[1 + b] + lax.broadcasted_iota(jnp.int32, (q.shape[0], count), 1)
                return pos < limit

            todo.append((k6, vv, visible))
        drafts = [
            jnp.concatenate(
                [ref[0, n, pl.ds(q_rows + which * heads + head, steps, stride=2 * heads), :] for ref, n in slots], axis=0
            )
            for which in range(2)
        ]

        def causal(count=drafts[0].shape[0]):
            row = lax.broadcasted_iota(jnp.int32, (q.shape[0], count), 0)
            col = lax.broadcasted_iota(jnp.int32, (q.shape[0], count), 1)
            return (row // rows == col // steps) & (col % steps <= row % rows // group)

        groups = in_pairs(todo)
        groups[0] = groups[0] + [(key_terms(drafts[0]), value_terms(drafts[1]), causal)]
        out = attend(q6, groups)
        for i in range(packets):
            for n in range(per):
                at = (i * per + n) * rows
                for step in range(steps):
                    first = step * heads * group + head * group
                    out_refs[i][0, n, first : first + group] = out[at + step * group : at + (step + 1) * group]


def decode_request(index, marks, packets, kv_list, carried, heads, group, steps, scale):
    nreq, per, packet_rows, dim = packets[0].shape
    blocks = len(kv_list)
    count = len(packets)
    q_rows = steps * heads * group
    pk_spec = pl.BlockSpec((1, per, packet_rows, dim), lambda i, m: (index, 0, 0, 0))
    out_spec = pl.BlockSpec((1, per, q_rows, dim), lambda i, m: (index, 0, 0, 0))
    kv_specs = [pl.BlockSpec(kv.shape, lambda i, m: (0, 0, 0, 0)) for kv in kv_list]
    extra_specs, extra, alias = [], [], {}
    if carried is not None:
        extra_specs, extra = [pl.BlockSpec(memory_space=pl.ANY)] * count, list(carried)
        alias = {1 + count + blocks + i: i for i in range(count)}
    keys = sum(kv.shape[2] for kv in kv_list)
    return pl.pallas_call(
        functools.partial(decode_kernel, blocks, count, heads, group, steps, scale),
        grid_spec=pltpu.PrefetchScalarGridSpec(
            num_scalar_prefetch=1,
            grid=(1,),
            in_specs=[pk_spec] * count + kv_specs + extra_specs,
            out_specs=[out_spec] * count,
        ),
        out_shape=[jax.ShapeDtypeStruct((nreq, per, q_rows, dim), F32)] * count,
        input_output_aliases=alias,
        compiler_params=pltpu.CompilerParams(vmem_limit_bytes=40 * 2**20),
        cost_estimate=pl.CostEstimate(
            flops=2 * 10 * count * per * steps * group * keys * dim,
            bytes_accessed=4 * (2 * count * per * packet_rows * dim + 2 * keys * dim),
            transcendentals=count * per * steps * group * keys,
        ),
        name="decode",
    )(marks, *packets, *kv_list, *extra)


def place_kernel(count, at, *refs):
    o_ref = refs[-1]
    nreq = refs[0].shape[0]
    for i in range(count):
        o_ref[pl.ds(at[i] * nreq, nreq)] = refs[i][...]


def place(at, pieces):
    nreq, per, rows, dim = pieces[0].shape
    count = len(pieces)
    return pl.pallas_call(
        functools.partial(place_kernel, count),
        in_specs=[pl.BlockSpec(memory_space=pltpu.SMEM)] + [pl.BlockSpec(memory_space=pltpu.VMEM)] * count,
        out_specs=pl.BlockSpec(memory_space=pltpu.VMEM),
        out_shape=jax.ShapeDtypeStruct((count * nreq, per, rows, dim), F32),
        name="place",
    )(at, *pieces)


def on_device(kv_cache, prefill_q, decode_q, decode_kv, lengths, row_length):
    ctx_count, head_count, rep_count = lax.axis_size("ctx"), lax.axis_size("head"), lax.axis_size("rep")
    ctx_index, head_index, rep_index = lax.axis_index("ctx"), lax.axis_index("head"), lax.axis_index("rep")
    nreq, _, block_len, heads, dim = kv_cache.shape
    span = prefill_q.shape[1]
    group = prefill_q.shape[2] // heads
    requests, per, steps, q_heads, _ = decode_q.shape
    scale = LOG2E / math.sqrt(dim)

    flat = kv_cache.reshape(nreq, 2, block_len * heads, dim)
    own = [flat[i : i + 1] for i in range(nreq)]
    shifts = range(1, ctx_count)
    held = [[own[i]] for i in range(nreq)]
    for shift in shifts:
        perm = [((i + shift) % ctx_count, i) for i in range(ctx_count)]
        for i in range(nreq):
            held[i].append(lax.ppermute(own[i], "ctx", perm))
    starts = jnp.stack([(ctx_index + shift) % ctx_count * block_len for shift in range(ctx_count)]).astype(jnp.int32)

    rows_f = jnp.broadcast_to(row_length.astype(F32)[:, :, None, None], (requests, per, 8, dim))
    packet = jnp.concatenate(
        [
            decode_q.reshape(requests, per, steps * q_heads, dim),
            decode_kv.reshape(requests, per, steps * 2 * heads, dim),
            rows_f,
        ],
        axis=2,
    )
    targets = [(rep_index + k) % head_count for k in range(head_count)]
    routes = [
        [(s * rep_count + t, (t + k) % head_count * rep_count + s) for s in range(head_count) for t in range(rep_count)]
        for k in range(head_count)
    ]
    packets = [
        lax.ppermute(lax.dynamic_slice_in_dim(packet, targets[k] * nreq, nreq, 0), ("head", "rep"), routes[k])
        for k in range(head_count)
    ]

    results = None
    prefill_out = None
    for i in range(nreq):
        length = lengths[head_index * nreq + i]
        first = length - span * ctx_count + ctx_index * span
        marks = jnp.concatenate([first[None].astype(jnp.int32), starts])
        results = decode_request(i, marks, packets, held[i], results, heads, group, steps, scale)
        prefill_out = prefill_request(i, marks, prefill_q, held[i], prefill_out, heads, scale)
    homes = [
        lax.ppermute(results[k], ("head", "rep"), [(b, a) for a, b in routes[k]]) for k in range(head_count)
    ]
    decode_out = place(jnp.stack(targets).astype(jnp.int32), homes).reshape(decode_q.shape)
    return (prefill_out, decode_out)


def solution(mesh):
    in_specs = (
        P("head", None, "ctx", "rep", None),
        P("head", "ctx", "rep", None),
        P(None, ("ctx", "rep"), None, "head", None),
        P(None, ("ctx", "rep"), None, None, "head", None),
        P(),
        P(None, ("ctx", "rep")),
    )
    out_specs = (P("head", "ctx", "rep", None), P(None, ("ctx", "rep"), None, "head", None))
    return jax.shard_map(on_device, mesh=mesh, in_specs=in_specs, out_specs=out_specs, check_vma=False)
```

```python
import functools
import math

import jax
import jax.numpy as jnp
from jax import lax
from jax.experimental import pallas as pl
from jax.experimental.pallas import tpu as pltpu
from jax.sharding import PartitionSpec as P

NEG_FILL = -1e30
LOG2E = math.log2(math.e)
F32 = jnp.float32
BF16 = jnp.bfloat16


def split_two(x):
    high = x.astype(BF16)
    return high, (x - high.astype(F32)).astype(BF16)


def split_three(x):
    high = x.astype(BF16)
    rest = x - high.astype(F32)
    mid = rest.astype(BF16)
    return high, mid, (rest - mid.astype(F32)).astype(BF16)


def query_terms(q):
    a, b, c = split_three(q)
    return jnp.concatenate([a, b, a, b, a, c], axis=-1)


def key_terms(k):
    a, b, c = split_three(k)
    return jnp.concatenate([a, a, b, b, c, a], axis=-1)


def value_terms(v):
    return jnp.concatenate(split_two(v), axis=-1)


def scores_of(q6, k6):
    return lax.dot_general(q6, k6, (((1,), (1,)), ((), ())), preferred_element_type=F32)


def weighted(p, vv):
    half = vv.shape[1] // 2
    a, b = split_two(p)
    both = jnp.dot(a, vv, preferred_element_type=F32) + jnp.dot(b, vv, preferred_element_type=F32)
    return both[:, :half] + both[:, half:]


def attend(q6, groups, state=None):
    for group in groups:
        parts = [jnp.where(mask(), scores_of(q6, k6), NEG_FILL) for k6, _, mask in group]
        top = functools.reduce(jnp.maximum, [jnp.max(s, axis=-1, keepdims=True) for s in parts])
        if state is not None:
            top = jnp.maximum(top, state[0])
        weights = [jnp.exp2(s - top) for s in parts]
        total = functools.reduce(jnp.add, [jnp.sum(w, axis=-1, keepdims=True) for w in weights])
        acc = functools.reduce(jnp.add, [weighted(w, vv) for w, (_, vv, _) in zip(weights, group)])
        if state is not None:
            factor = jnp.exp2(state[0] - top)
            total = total + state[1] * factor
            acc = acc + state[2] * factor
        state = (top, total, acc)
    return state


def put_state(state, acc_ref, stat_ref, at):
    top, total, acc = state
    acc_ref[at] = acc
    lane = lax.broadcasted_iota(jnp.int32, acc.shape, 1)
    stat_ref[at] = jnp.where(lane < acc.shape[1] // 2, top, total)


def get_state(acc_ref, stat_ref, at):
    stats = stat_ref[at]
    half = stats.shape[1] // 2
    return stats[:, 0:1], stats[:, half : half + 1], acc_ref[at]


def in_pairs(blocks):
    return [blocks[i : i + 2] for i in range(0, len(blocks), 2)]


def cache_head(ref, which, head, heads):
    rows = ref.shape[2] // heads
    return ref[0, which, pl.ds(head, rows, stride=heads), :]


def prefill_kernel(plan, heads, group, scale, marks, q_ref, *refs):
    blocks, first_block, started, finish, unread = plan
    kv_refs, refs = refs[:blocks], refs[blocks:]
    state_in = refs[:2] if started else None
    outs = refs[(2 if started else 0) + unread :]
    span = q_ref.shape[1]
    dim = q_ref.shape[3]
    head = pl.program_id(0)
    keys = [key_terms(cache_head(ref, 0, head, heads)) for ref in kv_refs]
    vals = [value_terms(cache_head(ref, 1, head, heads)) for ref in kv_refs]
    chunk = min(span, 64)
    for first in range(0, span, chunk):
        q = q_ref[0, first : first + chunk].reshape(chunk * group, dim) * scale
        q6 = query_terms(q)
        at = (0, pl.ds(first * group, chunk * group))

        def mask_of(b, first=first):
            shape = (chunk * group, keys[b].shape[0])
            pos = marks[1 + first_block + b] + lax.broadcasted_iota(jnp.int32, shape, 1)
            row = lax.broadcasted_iota(jnp.int32, shape, 0) // group
            return pos <= row + (marks[0] + first)

        todo = [(keys[b], vals[b], functools.partial(mask_of, b)) for b in range(blocks)]
        state = attend(q6, in_pairs(todo), get_state(*state_in, at) if started else None)
        if finish:
            outs[0][0, first : first + chunk] = (state[2] / state[1]).reshape(chunk, group, dim)
        else:
            put_state(state, outs[0], outs[1], at)
    if finish:
        outs[1][...] = jnp.zeros_like(outs[1])


def prefill_request(index, marks, prefill_q, kv_list, first_block, heads, scale, state=None, finish=True, carried=None, after=()):
    nreq, span, q_heads, dim = prefill_q.shape
    group = q_heads // heads
    blocks = len(kv_list)
    q_spec = pl.BlockSpec((1, span, group, dim), lambda k, m: (index, 0, k, 0))
    kv_specs = [pl.BlockSpec(kv.shape, lambda k, m: (0, 0, 0, 0)) for kv in kv_list]
    state_spec = pl.BlockSpec((1, span * group, dim), lambda k, m: (k, 0, 0))
    state_shape = jax.ShapeDtypeStruct((heads, span * group, dim), F32)
    started = state is not None
    state = list(state) if started else []
    unread = list(after) + ([carried] if carried is not None else [])
    alias = {2 + blocks + len(state) + len(after): 0} if carried is not None else {}
    keys = sum(kv.shape[2] for kv in kv_list) // heads
    if finish:
        out_specs = [q_spec, pl.BlockSpec((8, 128), lambda k, m: (0, 0))]
        out_shape = [jax.ShapeDtypeStruct(prefill_q.shape, F32), jax.ShapeDtypeStruct((8, 128), F32)]
    else:
        out_specs = [state_spec, state_spec]
        out_shape = [state_shape, state_shape]
    return pl.pallas_call(
        functools.partial(prefill_kernel, (blocks, first_block, started, finish, len(unread)), heads, group, scale),
        grid_spec=pltpu.PrefetchScalarGridSpec(
            num_scalar_prefetch=1,
            grid=(heads,),
            in_specs=[q_spec] + kv_specs + [state_spec] * len(state) + [pl.BlockSpec(memory_space=pl.ANY)] * len(unread),
            out_specs=out_specs,
        ),
        out_shape=out_shape,
        input_output_aliases=alias,
        compiler_params=pltpu.CompilerParams(vmem_limit_bytes=32 * 2**20),
        cost_estimate=pl.CostEstimate(
            flops=span * q_heads * keys * dim,
            bytes_accessed=4 * (2 * span * q_heads * dim + 2 * heads * keys * dim),
            transcendentals=span * q_heads * keys,
        ),
        name="prefill",
    )(marks, prefill_q, *kv_list, *state, *unread)


def decode_kernel(plan, heads, group, steps, scale, marks, *refs):
    packets, blocks, first_block, started, finish, unread = plan
    pk_refs, kv_refs, refs = refs[:packets], refs[packets : packets + blocks], refs[packets + blocks :]
    state_in = refs[:2] if started else None
    outs = refs[(2 if started else 0) + unread :]
    per = pk_refs[0].shape[1]
    dim = pk_refs[0].shape[3]
    q_rows = steps * heads * group
    rows = steps * group
    slots = [(ref, n) for ref in pk_refs for n in range(per)]
    at_limit = q_rows + 2 * heads * steps
    limit = jnp.concatenate(
        [jnp.broadcast_to(ref[0, n, at_limit : at_limit + 1, 0:1], (rows, 1)) for ref, n in slots], axis=0
    ).astype(jnp.int32)
    for head in range(heads):
        own = slice(head * group, (head + 1) * group)
        q = jnp.concatenate(
            [ref[0, n, 0:q_rows].reshape(steps, heads * group, dim)[:, own].reshape(rows, dim) for ref, n in slots], axis=0
        )
        q6 = query_terms(q * scale)
        todo = []
        for b, ref in enumerate(kv_refs):
            k6 = key_terms(cache_head(ref, 0, head, heads))
            vv = value_terms(cache_head(ref, 1, head, heads))

            def visible(b=b, count=k6.shape[0]):
                pos = marks[1 + first_block + b] + lax.broadcasted_iota(jnp.int32, (q.shape[0], count), 1)
                return pos < limit

            todo.append((k6, vv, visible))
        groups = in_pairs(todo)
        if not started:
            drafts = [
                jnp.concatenate(
                    [ref[0, n, pl.ds(q_rows + which * heads + head, steps, stride=2 * heads), :] for ref, n in slots], axis=0
                )
                for which in range(2)
            ]

            def causal(count=drafts[0].shape[0]):
                row = lax.broadcasted_iota(jnp.int32, (q.shape[0], count), 0)
                col = lax.broadcasted_iota(jnp.int32, (q.shape[0], count), 1)
                return (row // rows == col // steps) & (col % steps <= row % rows // group)

            groups[0] = groups[0] + [(key_terms(drafts[0]), value_terms(drafts[1]), causal)]
        state = attend(q6, groups, get_state(*state_in, head) if started else None)
        if not finish:
            put_state(state, outs[0], outs[1], head)
            continue
        out = state[2] / state[1]
        for i in range(packets):
            for n in range(per):
                at = (i * per + n) * rows
                for step in range(steps):
                    first = step * heads * group + head * group
                    outs[i][0, n, first : first + group] = out[at + step * group : at + (step + 1) * group]


def decode_request(
    index, marks, packets, kv_list, first_block, heads, group, steps, scale, state=None, finish=True, carried=None, after=()
):
    nreq, per, packet_rows, dim = packets[0].shape
    blocks = len(kv_list)
    count = len(packets)
    q_rows = steps * heads * group
    all_rows = count * per * steps * group
    pk_spec = pl.BlockSpec((1, per, packet_rows, dim), lambda i, m: (index, 0, 0, 0))
    out_spec = pl.BlockSpec((1, per, q_rows, dim), lambda i, m: (index, 0, 0, 0))
    kv_specs = [pl.BlockSpec(kv.shape, lambda i, m: (0, 0, 0, 0)) for kv in kv_list]
    state_spec = pl.BlockSpec((heads, all_rows, dim), lambda i, m: (0, 0, 0))
    started = state is not None
    state = list(state) if started else []
    unread = list(after) + (list(carried) if carried is not None else [])
    before = 1 + count + blocks + len(state) + len(after)
    alias = {before + i: i for i in range(count)} if carried is not None else {}
    if finish:
        out_specs = [out_spec] * count
        out_shape = [jax.ShapeDtypeStruct((nreq, per, q_rows, dim), F32)] * count
    else:
        out_specs = [state_spec] * 2
        out_shape = [jax.ShapeDtypeStruct((heads, all_rows, dim), F32)] * 2
    keys = sum(kv.shape[2] for kv in kv_list) // heads
    return pl.pallas_call(
        functools.partial(
            decode_kernel, (count, blocks, first_block, started, finish, len(unread)), heads, group, steps, scale
        ),
        grid_spec=pltpu.PrefetchScalarGridSpec(
            num_scalar_prefetch=1,
            grid=(1,),
            in_specs=[pk_spec] * count
            + kv_specs
            + [state_spec] * len(state)
            + [pl.BlockSpec(memory_space=pl.ANY)] * len(unread),
            out_specs=out_specs,
        ),
        out_shape=out_shape,
        input_output_aliases=alias,
        compiler_params=pltpu.CompilerParams(vmem_limit_bytes=16 * 2**20),
        cost_estimate=pl.CostEstimate(
            flops=all_rows * heads * keys * dim,
            bytes_accessed=4 * (2 * count * per * packet_rows * dim + 2 * heads * keys * dim),
            transcendentals=all_rows * heads * keys,
        ),
        name="decode",
    )(marks, *packets, *kv_list, *state, *unread)


def place_kernel(count, at, *refs):
    o_ref = refs[-1]
    nreq = refs[0].shape[0]
    for i in range(count):
        o_ref[pl.ds(at[i] * nreq, nreq)] = refs[i][...]


def place(at, pieces):
    nreq, per, rows, dim = pieces[0].shape
    count = len(pieces)
    return pl.pallas_call(
        functools.partial(place_kernel, count),
        in_specs=[pl.BlockSpec(memory_space=pltpu.SMEM)] + [pl.BlockSpec(memory_space=pltpu.VMEM)] * count,
        out_specs=pl.BlockSpec(memory_space=pltpu.VMEM),
        out_shape=jax.ShapeDtypeStruct((count * nreq, per, rows, dim), F32),
        compiler_params=pltpu.CompilerParams(vmem_limit_bytes=8 * 2**20),
        name="place",
    )(at, *pieces)


def on_device(kv_cache, prefill_q, decode_q, decode_kv, lengths, row_length):
    ctx_count, head_count, rep_count = lax.axis_size("ctx"), lax.axis_size("head"), lax.axis_size("rep")
    ctx_index, head_index, rep_index = lax.axis_index("ctx"), lax.axis_index("head"), lax.axis_index("rep")
    nreq, _, block_len, heads, dim = kv_cache.shape
    span = prefill_q.shape[1]
    group = prefill_q.shape[2] // heads
    requests, per, steps, q_heads, _ = decode_q.shape
    scale = LOG2E / math.sqrt(dim)

    flat = kv_cache.reshape(nreq, 2, block_len * heads, dim)
    own = [flat[i : i + 1] for i in range(nreq)]
    shifts = range(1, ctx_count)
    held = [[own[i]] for i in range(nreq)]
    for shift in shifts:
        perm = [((i + shift) % ctx_count, i) for i in range(ctx_count)]
        for i in range(nreq):
            held[i].append(lax.ppermute(own[i], "ctx", perm))
    starts = jnp.stack([(ctx_index + shift) % ctx_count * block_len for shift in range(ctx_count)]).astype(jnp.int32)

    rows_f = jnp.broadcast_to(row_length.astype(F32)[:, :, None, None], (requests, per, 8, dim))
    packet = jnp.concatenate(
        [
            decode_q.reshape(requests, per, steps * q_heads, dim),
            decode_kv.reshape(requests, per, steps * 2 * heads, dim),
            rows_f,
        ],
        axis=2,
    )
    targets = [(rep_index + k) % head_count for k in range(head_count)]
    routes = [
        [(s * rep_count + t, (t + k) % head_count * rep_count + s) for s in range(head_count) for t in range(rep_count)]
        for k in range(head_count)
    ]
    packets = [
        lax.ppermute(lax.dynamic_slice_in_dim(packet, targets[k] * nreq, nreq, 0), ("head", "rep"), routes[k])
        for k in range(head_count)
    ]

    def marks_of(i):
        length = lengths[head_index * nreq + i]
        first = length - span * ctx_count + ctx_index * span
        return jnp.concatenate([first[None].astype(jnp.int32), starts])

    last = nreq - 1
    last_marks = marks_of(last)
    prefill_state = prefill_request(last, last_marks, prefill_q, held[last][:1], 0, heads, scale, finish=False)
    results, prefill_out, token = None, None, None
    for i in range(last):
        marks = marks_of(i)
        prefill_out, token = prefill_request(i, marks, prefill_q, held[i], 0, heads, scale, carried=prefill_out)
        results = decode_request(i, marks, packets, held[i], 0, heads, group, steps, scale, carried=results)
    decode_state = decode_request(last, last_marks, packets, held[last][:1], 0, heads, group, steps, scale, finish=False)
    results = decode_request(
        last, last_marks, packets, held[last][1:], 1, heads, group, steps, scale,
        state=decode_state, carried=results, after=(token, prefill_state[0]),
    )
    prefill_out, _ = prefill_request(
        last, last_marks, prefill_q, held[last][1:], 1, heads, scale, state=prefill_state, carried=prefill_out
    )
    homes = [
        lax.ppermute(results[k], ("head", "rep"), [(b, a) for a, b in routes[k]]) for k in range(head_count)
    ]
    decode_out = place(jnp.stack(targets).astype(jnp.int32), homes).reshape(decode_q.shape)
    return (prefill_out, decode_out)


def solution(mesh):
    in_specs = (
        P("head", None, "ctx", "rep", None),
        P("head", "ctx", "rep", None),
        P(None, ("ctx", "rep"), None, "head", None),
        P(None, ("ctx", "rep"), None, None, "head", None),
        P(),
        P(None, ("ctx", "rep")),
    )
    out_specs = (P("head", "ctx", "rep", None), P(None, ("ctx", "rep"), None, "head", None))
    return jax.shard_map(on_device, mesh=mesh, in_specs=in_specs, out_specs=out_specs, check_vma=False)
```

```python
import functools
import math

import jax
import jax.numpy as jnp
from jax import lax
from jax.experimental import pallas as pl
from jax.experimental.pallas import tpu as pltpu
from jax.sharding import PartitionSpec as P

NEG_FILL = -1e30
LOG2E = math.log2(math.e)
F32 = jnp.float32
BF16 = jnp.bfloat16


def split_two(x):
    high = x.astype(BF16)
    return high, (x - high.astype(F32)).astype(BF16)


def split_three(x):
    high = x.astype(BF16)
    rest = x - high.astype(F32)
    mid = rest.astype(BF16)
    return high, mid, (rest - mid.astype(F32)).astype(BF16)


def query_terms(q):
    a, b, c = split_three(q)
    return jnp.concatenate([a, b, a, b, a, c], axis=-1)


def key_terms(k):
    a, b, c = split_three(k)
    return jnp.concatenate([a, a, b, b, c, a], axis=-1)


def value_terms(v):
    return jnp.concatenate(split_two(v.T), axis=0)


def score_block(k6, q6, limit, first_pos):
    s = lax.dot_general(k6, q6, (((1,), (1,)), ((), ())), preferred_element_type=F32)
    return jnp.where(lax.broadcasted_iota(jnp.int32, s.shape, 0) < limit - first_pos, s, NEG_FILL)


def weighted(vv, p):
    dim = vv.shape[0] // 2
    a, b = split_two(p)
    both = jnp.dot(vv, a, preferred_element_type=F32)
    return (both[:dim] + both[dim:]) + jnp.dot(vv[:dim], b, preferred_element_type=F32)


def fold(state, scores, values):
    top = functools.reduce(jnp.maximum, [jnp.max(s, axis=0, keepdims=True) for s in scores])
    if state is not None:
        top = jnp.maximum(top, state[0])
    weights = [jnp.exp2(s - top) for s in scores]
    total = functools.reduce(jnp.add, [jnp.sum(w, axis=0, keepdims=True) for w in weights])
    acc = functools.reduce(jnp.add, [weighted(vv, w) for vv, w in zip(values, weights)])
    if state is not None:
        factor = jnp.exp2(state[0] - top)
        total = total + state[1] * factor
        acc = acc + state[2] * factor
    return top, total, acc


def in_pairs(blocks):
    return [blocks[i : i + 2] for i in range(0, len(blocks), 2)]


def cache_head(ref, which, head, heads):
    return ref[0, which, pl.ds(head, ref.shape[2] // heads, stride=heads), :]


def put_state(state, acc_ref, stat_ref, head, cols):
    acc_ref[head, :, cols] = state[2]
    stat_ref[head, 0:1, cols] = state[0]
    stat_ref[head, 1:2, cols] = state[1]


def get_state(acc_ref, stat_ref, head, cols):
    return stat_ref[head, 0:1, cols], stat_ref[head, 1:2, cols], acc_ref[head, :, cols]


def state_shapes(heads, dim, rows):
    return [jax.ShapeDtypeStruct((heads, dim, rows), F32), jax.ShapeDtypeStruct((heads, 8, rows), F32)]


def block_starts(count, first, block_len):
    here, total = lax.axis_index("ctx"), lax.axis_size("ctx")
    return [lax.rem(here + (first + b), total) * block_len for b in range(count)]


def prefill_kernel(plan, heads, scale, lengths, q_ref, *refs):
    index, blocks, first_block, started, finish, unread = plan
    kv_refs, refs = refs[:blocks], refs[blocks:]
    state_in = refs[:2] if started else None
    outs = refs[(2 if started else 0) + unread :]
    _, span, q_heads, dim = q_ref.shape
    group = q_heads // heads
    chunk = min(span, CHUNK)
    total = lax.axis_size("ctx") * span
    begin = lengths[lax.axis_index("head") * q_ref.shape[0] + index] - total + lax.axis_index("ctx") * span
    at_pos = block_starts(blocks, first_block, kv_refs[0].shape[2] // heads)
    keys = [[key_terms(cache_head(ref, 0, h, heads)) for ref in kv_refs] for h in range(heads)]
    vals = [[value_terms(cache_head(ref, 1, h, heads)) for ref in kv_refs] for h in range(heads)]
    items = [(first, h) for first in range(0, span, chunk) for h in range(heads)]
    groups = in_pairs(list(range(blocks)))

    def scores(item):
        first, h = item
        q = q_ref[index, first : first + chunk, h * group : (h + 1) * group].reshape(chunk * group, dim) * scale
        q6 = query_terms(q)
        limit = begin + first + 1 + lax.broadcasted_iota(jnp.int32, (1, chunk * group), 1) // group
        return [
            functools.partial(
                lambda g: [score_block(keys[h][b], q6, limit, at_pos[b]) for b in g], g
            )
            for g in groups
        ]

    steps = [(n, g, make) for n, item in enumerate(items) for g, make in zip(groups, scores(item))]
    ahead = steps[0][2]()
    state = None
    copies = []
    for at, (n, g, _) in enumerate(steps):
        now, ahead = ahead, steps[at + 1][2]() if at + 1 < len(steps) else None
        first, h = items[n]
        cols = pl.ds(first * group, chunk * group)
        if g is groups[0]:
            state = get_state(*state_in, h, cols) if started else None
        state = fold(state, now, [vals[h][b] for b in g])
        if g is not groups[-1]:
            continue
        if not finish:
            put_state(state, outs[0], outs[1], h, cols)
            continue
        out_ref, hold, sems = outs[0], outs[-2], outs[-1]
        hold[n] = (state[2] * (1.0 / state[1])).T.reshape(chunk, group, dim)
        copy = pltpu.make_async_copy(
            hold.at[n], out_ref.at[index, pl.ds(first, chunk), pl.ds(h * group, group)], sems.at[n]
        )
        copy.start()
        copies.append(copy)
    if finish:
        outs[1][...] = jnp.zeros_like(outs[1])
    for copy in copies:
        copy.wait()


CHUNK = 64
SMEM_SPEC = pl.BlockSpec(memory_space=pltpu.SMEM)
VMEM_SPEC = pl.BlockSpec(memory_space=pltpu.VMEM)
ANY_SPEC = pl.BlockSpec(memory_space=pl.ANY)


def prefill_request(index, lengths, prefill_q, kv_list, first_block, heads, scale, state=None, finish=True, carried=None, after=()):
    nreq, span, q_heads, dim = prefill_q.shape
    group = q_heads // heads
    blocks = len(kv_list)
    started = state is not None
    state = list(state) if started else []
    unread = list(after) + ([carried] if carried is not None else [])
    alias = {2 + blocks + len(state) + len(after): 0} if carried is not None else {}
    keys = sum(kv.shape[2] for kv in kv_list) // heads
    scratch = []
    if finish:
        out_specs = [ANY_SPEC, VMEM_SPEC]
        out_shape = [jax.ShapeDtypeStruct(prefill_q.shape, F32), jax.ShapeDtypeStruct((8, 128), F32)]
        chunk = min(span, CHUNK)
        items = span // chunk * heads
        scratch = [pltpu.VMEM((items, chunk, group, dim), F32), pltpu.SemaphoreType.DMA((items,))]
    else:
        out_specs = [VMEM_SPEC, VMEM_SPEC]
        out_shape = state_shapes(heads, dim, span * group)
    return pl.pallas_call(
        functools.partial(prefill_kernel, (index, blocks, first_block, started, finish, len(unread)), heads, scale),
        in_specs=[SMEM_SPEC] + [VMEM_SPEC] * (1 + blocks + len(state)) + [ANY_SPEC] * len(unread),
        out_specs=out_specs,
        out_shape=out_shape,
        scratch_shapes=scratch,
        input_output_aliases=alias,
        compiler_params=pltpu.CompilerParams(vmem_limit_bytes=16 * 2**20),
        cost_estimate=pl.CostEstimate(
            flops=span * q_heads * keys * dim,
            bytes_accessed=4 * (2 * span * q_heads * dim + 2 * heads * keys * dim),
            transcendentals=span * q_heads * keys,
        ),
        name="prefill",
    )(lengths, prefill_q, *kv_list, *state, *unread)


def decode_kernel(plan, heads, group, steps, scale, *refs):
    index, near, blocks, first_block, started, finish, ready, unread = plan
    near_refs, far_ref, refs = refs[:near], refs[near], refs[near + 1 :]
    kv_refs, refs = refs[:blocks], refs[blocks:]
    state_in = refs[:2] if started else None
    refs = refs[2 if started else 0 :]
    ready_refs, outs = refs[:ready], refs[ready + unread :]
    side = lax.rem(lax.axis_index("head"), 2)
    at_pos = block_starts(blocks, first_block, kv_refs[0].shape[2] // heads)
    _, nreq, per, _, dim = far_ref.shape
    q_rows = steps * heads * group
    rows = steps * group
    slots = [(ref, side, n) for ref in near_refs for n in range(per)]
    slots += [(far_ref, j, n) for j in range(near) for n in range(per)]
    every = pl.ds(0, len(slots) * rows)
    at_limit = q_rows + 2 * heads * steps
    lane = lax.broadcasted_iota(jnp.int32, (1, len(slots) * rows), 1)
    limit = jnp.zeros(lane.shape, F32)
    for i, (ref, lead, n) in enumerate(slots):
        wide = jnp.broadcast_to(ref[lead, index, n, at_limit : at_limit + 1, 0:1], lane.shape)
        limit = jnp.where(lane // rows == i, wide, limit)
    limit = limit.astype(jnp.int32)
    if finish:
        for i in range(ready):
            first = i // 2
            outs[i % 2][:, first : first + 1] = ready_refs[i][...]
    for head in range(heads):
        own = slice(head * group, (head + 1) * group)
        q = jnp.concatenate(
            [
                ref[lead, index, n, 0:q_rows].reshape(steps, heads * group, dim)[:, own].reshape(rows, dim)
                for ref, lead, n in slots
            ],
            axis=0,
        )
        q6 = query_terms(q * scale)
        state = get_state(*state_in, head, every) if started else None
        for g, group_blocks in enumerate(in_pairs(list(range(blocks)))):
            parts = [
                score_block(key_terms(cache_head(kv_refs[b], 0, head, heads)), q6, limit, at_pos[b])
                for b in group_blocks
            ]
            vals = [value_terms(cache_head(kv_refs[b], 1, head, heads)) for b in group_blocks]
            if g == 0 and not started:
                drafts = [
                    jnp.concatenate(
                        [
                            ref[lead, index, n, pl.ds(q_rows + which * heads + head, steps, stride=2 * heads), :]
                            for ref, lead, n in slots
                        ],
                        axis=0,
                    )
                    for which in range(2)
                ]
                s = lax.dot_general(
                    key_terms(drafts[0]), q6, (((1,), (1,)), ((), ())), preferred_element_type=F32
                )
                key = lax.broadcasted_iota(jnp.int32, s.shape, 0)
                row = lax.broadcasted_iota(jnp.int32, s.shape, 1)
                seen = (row // rows == key // steps) & (key % steps <= row % rows // group)
                parts.append(jnp.where(seen, s, NEG_FILL))
                vals.append(value_terms(drafts[1]))
            state = fold(state, parts, vals)
        if not finish:
            put_state(state, outs[0], outs[1], head, every)
            continue
        out = (state[2] * (1.0 / state[1])).T
        for i in range(len(slots)):
            dst, j, n = outs[i // (near * per)], i // per % near, i % per
            for step in range(steps):
                first = step * heads * group + head * group
                at = i * rows + step * group
                dst[j, dst.shape[1] - 1, n, first : first + group] = out[at : at + group]


def decode_request(
    index, near, far, kv_list, first_block, heads, group, steps, scale, state=None, finish=True, ready=(), after=()
):
    count, _, per, packet_rows, dim = far.shape
    blocks = len(kv_list)
    q_rows = steps * heads * group
    all_rows = 2 * count * per * steps * group
    started = state is not None
    state = list(state) if started else []
    ready_flat = [a for one in ready for a in one]
    if finish:
        out_shape = [jax.ShapeDtypeStruct((count, len(ready) + 1, per, q_rows, dim), F32)] * 2
    else:
        out_shape = state_shapes(heads, dim, all_rows)
    keys = sum(kv.shape[2] for kv in kv_list) // heads
    plan = (index, count, blocks, first_block, started, finish, len(ready_flat), len(after))
    operands = count + 1 + blocks + len(state) + len(ready_flat)
    return pl.pallas_call(
        functools.partial(decode_kernel, plan, heads, group, steps, scale),
        in_specs=[VMEM_SPEC] * operands + [ANY_SPEC] * len(after),
        out_specs=[VMEM_SPEC] * len(out_shape),
        out_shape=out_shape,
        compiler_params=pltpu.CompilerParams(vmem_limit_bytes=12 * 2**20),
        cost_estimate=pl.CostEstimate(
            flops=all_rows * heads * keys * dim,
            bytes_accessed=4 * (4 * count * per * packet_rows * dim + 2 * heads * keys * dim),
            transcendentals=all_rows * heads * keys,
        ),
        name="decode",
    )(*near, far, *kv_list, *state, *ready_flat, *after)


def take_kernel(index, src, dst, sem):
    copy = pltpu.make_async_copy(src.at[pl.ds(index, 1)], dst, sem)
    copy.start()
    copy.wait()


def take(index, array):
    return pl.pallas_call(
        functools.partial(take_kernel, index),
        in_specs=[pl.BlockSpec(memory_space=pltpu.HBM)],
        out_specs=VMEM_SPEC,
        out_shape=jax.ShapeDtypeStruct((1,) + array.shape[1:], array.dtype),
        scratch_shapes=[pltpu.SemaphoreType.DMA],
        compiler_params=pltpu.CompilerParams(vmem_limit_bytes=4 * 2**20),
        name="take",
    )(array)


def pack_kernel(unread, lengths, q_ref, kv_ref, *refs):
    outs = refs[unread:]
    half = len(outs)
    _, nreq, per, rows, dim = outs[0].shape
    q_rows, kv_rows = q_ref.shape[2], kv_ref.shape[2]
    for j, out in enumerate(outs):
        pair = lax.rem(lax.axis_index("rep") + j, half)
        for c in range(2):
            for i in range(nreq):
                request = (pair * 2 + c) * nreq + i
                for n in range(per):
                    out[c, i, n, 0:q_rows] = q_ref[request, n]
                    out[c, i, n, q_rows : q_rows + kv_rows] = kv_ref[request, n]
                    reads = jnp.full((rows - q_rows - kv_rows, dim), lengths[request, n], jnp.int32)
                    out[c, i, n, q_rows + kv_rows :] = reads.astype(F32)


def pack(lengths, q, kv, half, nreq, after):
    requests, per, q_rows, dim = q.shape
    shape = jax.ShapeDtypeStruct((2, nreq, per, q_rows + kv.shape[2] + 8, dim), F32)
    return pl.pallas_call(
        functools.partial(pack_kernel, len(after)),
        in_specs=[SMEM_SPEC, VMEM_SPEC, VMEM_SPEC] + [ANY_SPEC] * len(after),
        out_specs=[VMEM_SPEC] * half,
        out_shape=[shape] * half,
        compiler_params=pltpu.CompilerParams(vmem_limit_bytes=4 * 2**20),
        cost_estimate=pl.CostEstimate(flops=10**11, bytes_accessed=10**6, transcendentals=0),
        name="pack",
    )(lengths, q, kv, *after)


def other_kernel(count, *refs):
    out = refs[-1]
    for j, ref in enumerate(refs[:count]):
        out[j] = ref[1 - lax.rem(lax.axis_index("head"), 2)]


def other_side(near, after):
    return pl.pallas_call(
        functools.partial(other_kernel, len(near)),
        in_specs=[VMEM_SPEC] * len(near) + [ANY_SPEC] * len(after),
        out_specs=VMEM_SPEC,
        out_shape=jax.ShapeDtypeStruct((len(near),) + near[0].shape[1:], F32),
        compiler_params=pltpu.CompilerParams(vmem_limit_bytes=4 * 2**20),
        name="other_side",
    )(*near, *after)


def join_kernel(kept, back, *outs):
    side = lax.rem(lax.axis_index("head"), 2)
    for j, out in enumerate(outs):
        out[side] = kept[j]
        out[1 - side] = back[j]


def join(kept, back):
    count = kept.shape[0]
    return pl.pallas_call(
        join_kernel,
        in_specs=[VMEM_SPEC] * 2,
        out_specs=[VMEM_SPEC] * count,
        out_shape=[jax.ShapeDtypeStruct((2,) + kept.shape[1:], F32)] * count,
        compiler_params=pltpu.CompilerParams(vmem_limit_bytes=4 * 2**20),
        name="join",
    )(kept, back)


def place_kernel(*refs):
    o_ref, count = refs[-1], len(refs) - 1
    size = refs[0].shape[0]
    for j in range(count):
        o_ref[pl.ds(lax.rem(lax.axis_index("rep") + j, count) * size, size)] = refs[j][...]


def place(pieces):
    size, per, rows, dim = pieces[0].shape
    count = len(pieces)
    return pl.pallas_call(
        place_kernel,
        in_specs=[VMEM_SPEC] * count,
        out_specs=VMEM_SPEC,
        out_shape=jax.ShapeDtypeStruct((count * size, per, rows, dim), F32),
        compiler_params=pltpu.CompilerParams(vmem_limit_bytes=4 * 2**20),
        name="place",
    )(*pieces)


def on_device(kv_cache, prefill_q, decode_q, decode_kv, lengths, row_length):
    ctx_count, head_count, rep_count = lax.axis_size("ctx"), lax.axis_size("head"), lax.axis_size("rep")
    nreq, _, block_len, heads, dim = kv_cache.shape
    group = prefill_q.shape[2] // heads
    requests, per, steps, q_heads, _ = decode_q.shape
    scale = LOG2E / math.sqrt(dim)
    half = head_count // 2

    flat = kv_cache.reshape(nreq, 2, block_len * heads, dim)
    own = [take(i, flat) for i in range(nreq)]
    held = [[own[i]] for i in range(nreq)]
    for shift in range(1, ctx_count):
        perm = [((i + shift) % ctx_count, i) for i in range(ctx_count)]
        for i in range(nreq):
            held[i].append(lax.ppermute(own[i], "ctx", perm))

    routes = [
        [
            (s * rep_count + t, ((t + j) % half * 2 + t // half) * rep_count + s)
            for s in range(head_count)
            for t in range(rep_count)
        ]
        for j in range(half)
    ]
    swap = [(i, i ^ 1) for i in range(head_count)]
    packets = pack(
        row_length,
        decode_q.reshape(requests, per, steps * q_heads, dim),
        decode_kv.reshape(requests, per, steps * 2 * heads, dim),
        half,
        nreq,
        own,
    )
    near = [lax.ppermute(packets[j], ("head", "rep"), routes[j]) for j in range(half)]
    last = nreq - 1
    prefill_state = prefill_request(last, lengths, prefill_q, held[last][:1], 0, heads, scale, finish=False, after=packets[:1])
    prefill_out, token = None, prefill_state[1]
    for i in range(last):
        prefill_out, token = prefill_request(i, lengths, prefill_q, held[i], 0, heads, scale, carried=prefill_out, after=(token,))
    far = lax.ppermute(other_side(near, (token,)), "head", swap)
    ready = [decode_request(i, near, far, held[i], 0, heads, group, steps, scale) for i in range(last)]
    decode_state = decode_request(last, near, far, held[last][:1], 0, heads, group, steps, scale, finish=False)
    kept, sent = decode_request(
        last, near, far, held[last][1:], 1, heads, group, steps, scale, state=decode_state, ready=ready
    )
    prefill_out, _ = prefill_request(
        last, lengths, prefill_q, held[last][1:], 1, heads, scale, state=prefill_state, carried=prefill_out
    )
    joined = join(kept, lax.ppermute(sent, "head", swap))
    homes = [lax.ppermute(joined[j], ("head", "rep"), [(b, a) for a, b in routes[j]]) for j in range(half)]
    decode_out = place([a.reshape((2 * nreq,) + a.shape[2:]) for a in homes]).reshape(decode_q.shape)
    return (prefill_out, decode_out)


def solution(mesh):
    in_specs = (
        P("head", None, "ctx", "rep", None),
        P("head", "ctx", "rep", None),
        P(None, ("ctx", "rep"), None, "head", None),
        P(None, ("ctx", "rep"), None, None, "head", None),
        P(),
        P(None, ("ctx", "rep")),
    )
    out_specs = (P("head", "ctx", "rep", None), P(None, ("ctx", "rep"), None, "head", None))
    return jax.shard_map(on_device, mesh=mesh, in_specs=in_specs, out_specs=out_specs, check_vma=False)
```

```python
import functools
import math

import jax
import jax.numpy as jnp
from jax import lax
from jax.experimental import pallas as pl
from jax.experimental.pallas import tpu as pltpu
from jax.sharding import PartitionSpec as P

NEG_FILL = -1e30
LOG2E = math.log2(math.e)
F32 = jnp.float32
BF16 = jnp.bfloat16


def split_two(x):
    high = x.astype(BF16)
    return high, (x - high.astype(F32)).astype(BF16)


def split_three(x):
    high = x.astype(BF16)
    rest = x - high.astype(F32)
    mid = rest.astype(BF16)
    return high, mid, (rest - mid.astype(F32)).astype(BF16)


def query_terms(q):
    a, b, c = split_three(q)
    return jnp.concatenate([a, b, a, b, a, c], axis=-1)


def key_terms(k):
    a, b, c = split_three(k)
    return jnp.concatenate([a, a, b, b, c, a], axis=-1)


def value_terms(v):
    return jnp.concatenate(split_two(v.T), axis=0)


def score_block(k6, q6, limit, first_pos):
    s = lax.dot_general(k6, q6, (((1,), (1,)), ((), ())), preferred_element_type=F32)
    return jnp.where(lax.broadcasted_iota(jnp.int32, s.shape, 0) < limit - first_pos, s, NEG_FILL)


def weighted(vv, p):
    dim = vv.shape[0] // 2
    a, b = split_two(p)
    both = jnp.dot(vv, a, preferred_element_type=F32)
    return (both[:dim] + both[dim:]) + jnp.dot(vv[:dim], b, preferred_element_type=F32)


def fold(state, scores, values):
    top = functools.reduce(jnp.maximum, [jnp.max(s, axis=0, keepdims=True) for s in scores])
    if state is not None:
        top = jnp.maximum(top, state[0])
    weights = [jnp.exp2(s - top) for s in scores]
    total = functools.reduce(jnp.add, [jnp.sum(w, axis=0, keepdims=True) for w in weights])
    acc = functools.reduce(jnp.add, [weighted(vv, w) for vv, w in zip(values, weights)])
    if state is not None:
        factor = jnp.exp2(state[0] - top)
        total = total + state[1] * factor
        acc = acc + state[2] * factor
    return top, total, acc


def in_pairs(blocks):
    return [blocks[i : i + 2] for i in range(0, len(blocks), 2)]


def cache_head(ref, which, head, heads):
    return ref[0, which, pl.ds(head, ref.shape[2] // heads, stride=heads), :]


def put_state(state, acc_ref, stat_ref, head, cols):
    acc_ref[head, :, cols] = state[2]
    stat_ref[head, 0:1, cols] = state[0]
    stat_ref[head, 1:2, cols] = state[1]


def get_state(acc_ref, stat_ref, head, cols):
    return stat_ref[head, 0:1, cols], stat_ref[head, 1:2, cols], acc_ref[head, :, cols]


def state_shapes(heads, dim, rows):
    return [jax.ShapeDtypeStruct((heads, dim, rows), F32), jax.ShapeDtypeStruct((heads, 8, rows), F32)]


def block_starts(count, first, block_len):
    here, total = lax.axis_index("ctx"), lax.axis_size("ctx")
    return [lax.rem(here + (first + b), total) * block_len for b in range(count)]


def prefill_kernel(plan, heads, scale, lengths, q_ref, *refs):
    index, blocks, first_block, started, finish, unread = plan
    kv_refs, refs = refs[:blocks], refs[blocks:]
    state_in = refs[:2] if started else None
    outs = refs[(2 if started else 0) + unread :]
    _, span, q_heads, dim = q_ref.shape
    group = q_heads // heads
    chunk = min(span, CHUNK)
    total = lax.axis_size("ctx") * span
    begin = lengths[lax.axis_index("head") * q_ref.shape[0] + index] - total + lax.axis_index("ctx") * span
    at_pos = block_starts(blocks, first_block, kv_refs[0].shape[2] // heads)
    keys = [[key_terms(cache_head(ref, 0, h, heads)) for ref in kv_refs] for h in range(heads)]
    vals = [[value_terms(cache_head(ref, 1, h, heads)) for ref in kv_refs] for h in range(heads)]
    items = [(first, h) for first in range(0, span, chunk) for h in range(heads)]
    groups = in_pairs(list(range(blocks)))

    def scores(item):
        first, h = item
        q = q_ref[index, first : first + chunk, h * group : (h + 1) * group].reshape(chunk * group, dim) * scale
        q6 = query_terms(q)
        limit = begin + first + 1 + lax.broadcasted_iota(jnp.int32, (1, chunk * group), 1) // group
        return [
            functools.partial(
                lambda g: [score_block(keys[h][b], q6, limit, at_pos[b]) for b in g], g
            )
            for g in groups
        ]

    steps = [(n, g, make) for n, item in enumerate(items) for g, make in zip(groups, scores(item))]
    ahead = steps[0][2]()
    state = None
    copies = []
    for at, (n, g, _) in enumerate(steps):
        now, ahead = ahead, steps[at + 1][2]() if at + 1 < len(steps) else None
        first, h = items[n]
        cols = pl.ds(first * group, chunk * group)
        if g is groups[0]:
            state = get_state(*state_in, h, cols) if started else None
        state = fold(state, now, [vals[h][b] for b in g])
        if g is not groups[-1]:
            continue
        if not finish:
            put_state(state, outs[0], outs[1], h, cols)
            continue
        out_ref, hold, sems = outs[0], outs[-2], outs[-1]
        hold[n] = (state[2] * (1.0 / state[1])).T.reshape(chunk, group, dim)
        copy = pltpu.make_async_copy(
            hold.at[n], out_ref.at[index, pl.ds(first, chunk), pl.ds(h * group, group)], sems.at[n]
        )
        copy.start()
        copies.append(copy)
    if finish:
        outs[1][...] = jnp.zeros_like(outs[1])
    for copy in copies:
        copy.wait()


CHUNK = 64
SMEM_SPEC = pl.BlockSpec(memory_space=pltpu.SMEM)
VMEM_SPEC = pl.BlockSpec(memory_space=pltpu.VMEM)
ANY_SPEC = pl.BlockSpec(memory_space=pl.ANY)


def prefill_request(index, lengths, prefill_q, kv_list, first_block, heads, scale, state=None, finish=True, carried=None, after=()):
    nreq, span, q_heads, dim = prefill_q.shape
    group = q_heads // heads
    blocks = len(kv_list)
    started = state is not None
    state = list(state) if started else []
    unread = list(after) + ([carried] if carried is not None else [])
    alias = {2 + blocks + len(state) + len(after): 0} if carried is not None else {}
    keys = sum(kv.shape[2] for kv in kv_list) // heads
    scratch = []
    if finish:
        out_specs = [ANY_SPEC, VMEM_SPEC]
        out_shape = [jax.ShapeDtypeStruct(prefill_q.shape, F32), jax.ShapeDtypeStruct((8, 128), F32)]
        chunk = min(span, CHUNK)
        items = span // chunk * heads
        scratch = [pltpu.VMEM((items, chunk, group, dim), F32), pltpu.SemaphoreType.DMA((items,))]
    else:
        out_specs = [VMEM_SPEC, VMEM_SPEC]
        out_shape = state_shapes(heads, dim, span * group)
    return pl.pallas_call(
        functools.partial(prefill_kernel, (index, blocks, first_block, started, finish, len(unread)), heads, scale),
        in_specs=[SMEM_SPEC] + [VMEM_SPEC] * (1 + blocks + len(state)) + [ANY_SPEC] * len(unread),
        out_specs=out_specs,
        out_shape=out_shape,
        scratch_shapes=scratch,
        input_output_aliases=alias,
        compiler_params=pltpu.CompilerParams(vmem_limit_bytes=16 * 2**20),
        cost_estimate=pl.CostEstimate(
            flops=span * q_heads * keys * dim,
            bytes_accessed=4 * (2 * span * q_heads * dim + 2 * heads * keys * dim),
            transcendentals=span * q_heads * keys,
        ),
        name="prefill",
    )(lengths, prefill_q, *kv_list, *state, *unread)


def decode_kernel(plan, heads, group, steps, scale, *refs):
    index, near, blocks, first_block, started, finish, ready, unread = plan
    near_refs, far_ref, refs = refs[:near], refs[near], refs[near + 1 :]
    kv_refs, refs = refs[:blocks], refs[blocks:]
    state_in = refs[:2] if started else None
    refs = refs[2 if started else 0 :]
    ready_refs, outs = refs[:ready], refs[ready + unread :]
    side = lax.rem(lax.axis_index("head"), 2)
    at_pos = block_starts(blocks, first_block, kv_refs[0].shape[2] // heads)
    _, nreq, per, _, dim = far_ref.shape
    q_rows = steps * heads * group
    rows = steps * group
    slots = [(ref, side, n) for ref in near_refs for n in range(per)]
    slots += [(far_ref, j, n) for j in range(near) for n in range(per)]
    every = pl.ds(0, len(slots) * rows)
    at_limit = q_rows + 2 * heads * steps
    lane = lax.broadcasted_iota(jnp.int32, (1, len(slots) * rows), 1)
    limit = jnp.zeros(lane.shape, F32)
    for i, (ref, lead, n) in enumerate(slots):
        wide = jnp.broadcast_to(ref[lead, index, n, at_limit : at_limit + 1, 0:1], lane.shape)
        limit = jnp.where(lane // rows == i, wide, limit)
    limit = limit.astype(jnp.int32)
    if finish:
        for i in range(ready):
            first = i // 2
            outs[i % 2][:, first : first + 1] = ready_refs[i][...]
    for head in range(heads):
        own = slice(head * group, (head + 1) * group)
        q = jnp.concatenate(
            [
                ref[lead, index, n, 0:q_rows].reshape(steps, heads * group, dim)[:, own].reshape(rows, dim)
                for ref, lead, n in slots
            ],
            axis=0,
        )
        q6 = query_terms(q * scale)
        state = get_state(*state_in, head, every) if started else None
        for g, group_blocks in enumerate(in_pairs(list(range(blocks)))):
            parts = [
                score_block(key_terms(cache_head(kv_refs[b], 0, head, heads)), q6, limit, at_pos[b])
                for b in group_blocks
            ]
            vals = [value_terms(cache_head(kv_refs[b], 1, head, heads)) for b in group_blocks]
            if g == 0 and not started:
                drafts = [
                    jnp.concatenate(
                        [
                            ref[lead, index, n, pl.ds(q_rows + which * heads + head, steps, stride=2 * heads), :]
                            for ref, lead, n in slots
                        ],
                        axis=0,
                    )
                    for which in range(2)
                ]
                s = lax.dot_general(
                    key_terms(drafts[0]), q6, (((1,), (1,)), ((), ())), preferred_element_type=F32
                )
                key = lax.broadcasted_iota(jnp.int32, s.shape, 0)
                row = lax.broadcasted_iota(jnp.int32, s.shape, 1)
                seen = (row // rows == key // steps) & (key % steps <= row % rows // group)
                parts.append(jnp.where(seen, s, NEG_FILL))
                vals.append(value_terms(drafts[1]))
            state = fold(state, parts, vals)
        if not finish:
            put_state(state, outs[0], outs[1], head, every)
            continue
        out = (state[2] * (1.0 / state[1])).T
        for i in range(len(slots)):
            dst, j, n = outs[i // (near * per)], i // per % near, i % per
            for step in range(steps):
                first = step * heads * group + head * group
                at = i * rows + step * group
                dst[j, dst.shape[1] - 1, n, first : first + group] = out[at : at + group]


def decode_request(
    index, near, far, kv_list, first_block, heads, group, steps, scale, state=None, finish=True, ready=(), after=()
):
    count, _, per, packet_rows, dim = far.shape
    blocks = len(kv_list)
    q_rows = steps * heads * group
    all_rows = 2 * count * per * steps * group
    started = state is not None
    state = list(state) if started else []
    ready_flat = [a for one in ready for a in one]
    if finish:
        out_shape = [jax.ShapeDtypeStruct((count, len(ready) + 1, per, q_rows, dim), F32)] * 2
    else:
        out_shape = state_shapes(heads, dim, all_rows)
    keys = sum(kv.shape[2] for kv in kv_list) // heads
    plan = (index, count, blocks, first_block, started, finish, len(ready_flat), len(after))
    operands = count + 1 + blocks + len(state) + len(ready_flat)
    return pl.pallas_call(
        functools.partial(decode_kernel, plan, heads, group, steps, scale),
        in_specs=[VMEM_SPEC] * operands + [ANY_SPEC] * len(after),
        out_specs=[VMEM_SPEC] * len(out_shape),
        out_shape=out_shape,
        compiler_params=pltpu.CompilerParams(vmem_limit_bytes=12 * 2**20),
        cost_estimate=pl.CostEstimate(
            flops=all_rows * heads * keys * dim,
            bytes_accessed=4 * (4 * count * per * packet_rows * dim + 2 * heads * keys * dim),
            transcendentals=all_rows * heads * keys,
        ),
        name="decode",
    )(*near, far, *kv_list, *state, *ready_flat, *after)


def take_kernel(index, src, dst, sem):
    copy = pltpu.make_async_copy(src.at[pl.ds(index, 1)], dst, sem)
    copy.start()
    copy.wait()


def take(index, array):
    return pl.pallas_call(
        functools.partial(take_kernel, index),
        in_specs=[pl.BlockSpec(memory_space=pltpu.HBM)],
        out_specs=VMEM_SPEC,
        out_shape=jax.ShapeDtypeStruct((1,) + array.shape[1:], array.dtype),
        scratch_shapes=[pltpu.SemaphoreType.DMA],
        compiler_params=pltpu.CompilerParams(vmem_limit_bytes=4 * 2**20),
        name="take",
    )(array)


def pack_kernel(unread, lengths, q_ref, kv_ref, *refs):
    outs = refs[unread:]
    half = len(outs)
    _, nreq, per, rows, dim = outs[0].shape
    q_rows, kv_rows = q_ref.shape[2], kv_ref.shape[2]
    for j, out in enumerate(outs):
        pair = lax.rem(lax.axis_index("rep") + (j + 1), half)
        for c in range(2):
            for i in range(nreq):
                request = (pair * 2 + c) * nreq + i
                for n in range(per):
                    out[c, i, n, 0:q_rows] = q_ref[request, n]
                    out[c, i, n, q_rows : q_rows + kv_rows] = kv_ref[request, n]
                    reads = jnp.full((rows - q_rows - kv_rows, dim), lengths[request, n], jnp.int32)
                    out[c, i, n, q_rows + kv_rows :] = reads.astype(F32)


def pack(lengths, q, kv, half, nreq, after):
    requests, per, q_rows, dim = q.shape
    shape = jax.ShapeDtypeStruct((2, nreq, per, q_rows + kv.shape[2] + 8, dim), F32)
    return pl.pallas_call(
        functools.partial(pack_kernel, len(after)),
        in_specs=[SMEM_SPEC, VMEM_SPEC, VMEM_SPEC] + [ANY_SPEC] * len(after),
        out_specs=[VMEM_SPEC] * half,
        out_shape=[shape] * half,
        compiler_params=pltpu.CompilerParams(vmem_limit_bytes=4 * 2**20),
        cost_estimate=pl.CostEstimate(flops=10**11, bytes_accessed=10**6, transcendentals=0),
        name="pack",
    )(lengths, q, kv, *after)


def other_kernel(count, *refs):
    out = refs[-1]
    for j, ref in enumerate(refs[:count]):
        out[j] = ref[1 - lax.rem(lax.axis_index("head"), 2)]


def other_side(near, after):
    return pl.pallas_call(
        functools.partial(other_kernel, len(near)),
        in_specs=[VMEM_SPEC] * len(near) + [ANY_SPEC] * len(after),
        out_specs=VMEM_SPEC,
        out_shape=jax.ShapeDtypeStruct((len(near),) + near[0].shape[1:], F32),
        compiler_params=pltpu.CompilerParams(vmem_limit_bytes=4 * 2**20),
        name="other_side",
    )(*near, *after)


def join_kernel(kept, back, *outs):
    side = lax.rem(lax.axis_index("head"), 2)
    for j, out in enumerate(outs):
        out[side] = kept[j]
        out[1 - side] = back[j]


def join(kept, back):
    count = kept.shape[0]
    return pl.pallas_call(
        join_kernel,
        in_specs=[VMEM_SPEC] * 2,
        out_specs=[VMEM_SPEC] * count,
        out_shape=[jax.ShapeDtypeStruct((2,) + kept.shape[1:], F32)] * count,
        compiler_params=pltpu.CompilerParams(vmem_limit_bytes=4 * 2**20),
        name="join",
    )(kept, back)


def place_kernel(*refs):
    o_ref, count = refs[-1], len(refs) - 1
    size = refs[0].shape[0]
    for j in range(count):
        o_ref[pl.ds(lax.rem(lax.axis_index("rep") + (j + 1), count) * size, size)] = refs[j][...]


def place(pieces):
    size, per, rows, dim = pieces[0].shape
    count = len(pieces)
    return pl.pallas_call(
        place_kernel,
        in_specs=[VMEM_SPEC] * count,
        out_specs=VMEM_SPEC,
        out_shape=jax.ShapeDtypeStruct((count * size, per, rows, dim), F32),
        compiler_params=pltpu.CompilerParams(vmem_limit_bytes=4 * 2**20),
        name="place",
    )(*pieces)


def on_device(kv_cache, prefill_q, decode_q, decode_kv, lengths, row_length):
    ctx_count, head_count, rep_count = lax.axis_size("ctx"), lax.axis_size("head"), lax.axis_size("rep")
    nreq, _, block_len, heads, dim = kv_cache.shape
    group = prefill_q.shape[2] // heads
    requests, per, steps, q_heads, _ = decode_q.shape
    scale = LOG2E / math.sqrt(dim)
    half = head_count // 2

    flat = kv_cache.reshape(nreq, 2, block_len * heads, dim)
    own = [take(i, flat) for i in range(nreq)]
    held = [[own[i]] for i in range(nreq)]
    for shift in range(1, ctx_count):
        perm = [((i + shift) % ctx_count, i) for i in range(ctx_count)]
        for i in range(nreq):
            held[i].append(lax.ppermute(own[i], "ctx", perm))

    routes = [
        [
            (s * rep_count + t, ((t + j + 1) % half * 2 + t // half) * rep_count + s)
            for s in range(head_count)
            for t in range(rep_count)
        ]
        for j in range(half)
    ]
    swap = [(i, i ^ 1) for i in range(head_count)]
    packets = pack(
        row_length,
        decode_q.reshape(requests, per, steps * q_heads, dim),
        decode_kv.reshape(requests, per, steps * 2 * heads, dim),
        half,
        nreq,
        own,
    )
    near = [lax.ppermute(packets[j], ("head", "rep"), routes[j]) for j in range(half)]
    last = nreq - 1
    prefill_state = prefill_request(last, lengths, prefill_q, held[last][:1], 0, heads, scale, finish=False, after=packets[:1])
    prefill_out, token = None, prefill_state[1]
    for i in range(last):
        prefill_out, token = prefill_request(i, lengths, prefill_q, held[i], 0, heads, scale, carried=prefill_out, after=(token,))
    far = lax.ppermute(other_side(near, (token,)), "head", swap)
    ready = [decode_request(i, near, far, held[i], 0, heads, group, steps, scale) for i in range(last)]
    decode_state = decode_request(last, near, far, held[last][:1], 0, heads, group, steps, scale, finish=False)
    kept, sent = decode_request(
        last, near, far, held[last][1:], 1, heads, group, steps, scale, state=decode_state, ready=ready
    )
    prefill_out, _ = prefill_request(
        last, lengths, prefill_q, held[last][1:], 1, heads, scale, state=prefill_state, carried=prefill_out
    )
    joined = join(kept, lax.ppermute(sent, "head", swap))
    homes = [lax.ppermute(joined[j], ("head", "rep"), [(b, a) for a, b in routes[j]]) for j in range(half)]
    decode_out = place([a.reshape((2 * nreq,) + a.shape[2:]) for a in homes]).reshape(decode_q.shape)
    return (prefill_out, decode_out)


def solution(mesh):
    in_specs = (
        P("head", None, "ctx", "rep", None),
        P("head", "ctx", "rep", None),
        P(None, ("ctx", "rep"), None, "head", None),
        P(None, ("ctx", "rep"), None, None, "head", None),
        P(),
        P(None, ("ctx", "rep")),
    )
    out_specs = (P("head", "ctx", "rep", None), P(None, ("ctx", "rep"), None, "head", None))
    return jax.shard_map(on_device, mesh=mesh, in_specs=in_specs, out_specs=out_specs, check_vma=False)
```

```python
import functools
import math

import jax
import jax.numpy as jnp
from jax import lax
from jax.experimental import pallas as pl
from jax.experimental.pallas import tpu as pltpu
from jax.sharding import PartitionSpec as P

NEG_FILL = -1e30
LOG2E = math.log2(math.e)
F32 = jnp.float32
BF16 = jnp.bfloat16


def split_two(x):
    high = x.astype(BF16)
    return high, (x - high.astype(F32)).astype(BF16)


def split_three(x):
    high = x.astype(BF16)
    rest = x - high.astype(F32)
    mid = rest.astype(BF16)
    return high, mid, (rest - mid.astype(F32)).astype(BF16)


def query_terms(q):
    a, b, c = split_three(q)
    return jnp.concatenate([a, b, a, b, a, c], axis=-1)


def key_terms(k):
    a, b, c = split_three(k)
    return jnp.concatenate([a, a, b, b, c, a], axis=-1)


def value_terms(v):
    return jnp.concatenate(split_two(v.T), axis=0)


def score_block(k6, q6, limit, first_pos):
    s = lax.dot_general(k6, q6, (((1,), (1,)), ((), ())), preferred_element_type=F32)
    return jnp.where(lax.broadcasted_iota(jnp.int32, s.shape, 0) < limit - first_pos, s, NEG_FILL)


def weighted(vv, p):
    dim = vv.shape[0] // 2
    a, b = split_two(p)
    both = jnp.dot(vv, a, preferred_element_type=F32)
    return (both[:dim] + both[dim:]) + jnp.dot(vv[:dim], b, preferred_element_type=F32)


def fold(state, scores, values):
    top = functools.reduce(jnp.maximum, [jnp.max(s, axis=0, keepdims=True) for s in scores])
    if state is not None:
        top = jnp.maximum(top, state[0])
    weights = [jnp.exp2(s - top) for s in scores]
    total = functools.reduce(jnp.add, [jnp.sum(w, axis=0, keepdims=True) for w in weights])
    acc = functools.reduce(jnp.add, [weighted(vv, w) for vv, w in zip(values, weights)])
    if state is not None:
        factor = jnp.exp2(state[0] - top)
        total = total + state[1] * factor
        acc = acc + state[2] * factor
    return top, total, acc


def in_pairs(blocks):
    return [blocks[i : i + 2] for i in range(0, len(blocks), 2)]


def cache_head(ref, which, head, heads):
    return ref[0, which, pl.ds(head, ref.shape[2] // heads, stride=heads), :]


def put_state(state, acc_ref, stat_ref, head, cols):
    acc_ref[head, :, cols] = state[2]
    stat_ref[head, 0:1, cols] = state[0]
    stat_ref[head, 1:2, cols] = state[1]


def get_state(acc_ref, stat_ref, head, cols):
    return stat_ref[head, 0:1, cols], stat_ref[head, 1:2, cols], acc_ref[head, :, cols]


def state_shapes(heads, dim, rows):
    return [jax.ShapeDtypeStruct((heads, dim, rows), F32), jax.ShapeDtypeStruct((heads, 8, rows), F32)]


def pair_of(t, j, half):
    return (t // 2 + j + 1) % half


def core_of(t, half):
    return (t + t // 2) % 2


def block_starts(count, first, block_len):
    here, total = lax.axis_index("ctx"), lax.axis_size("ctx")
    return [lax.rem(here + (first + b), total) * block_len for b in range(count)]


def prefill_kernel(plan, heads, scale, lengths, q_ref, *refs):
    index, blocks, first_block, started, finish, unread = plan
    kv_refs, refs = refs[:blocks], refs[blocks:]
    state_in = refs[:2] if started else None
    outs = refs[(2 if started else 0) + unread :]
    _, span, q_heads, dim = q_ref.shape
    group = q_heads // heads
    chunk = min(span, CHUNK)
    total = lax.axis_size("ctx") * span
    begin = lengths[lax.axis_index("head") * q_ref.shape[0] + index] - total + lax.axis_index("ctx") * span
    at_pos = block_starts(blocks, first_block, kv_refs[0].shape[2] // heads)
    keys = [[key_terms(cache_head(ref, 0, h, heads)) for ref in kv_refs] for h in range(heads)]
    vals = [[value_terms(cache_head(ref, 1, h, heads)) for ref in kv_refs] for h in range(heads)]
    items = [(first, h) for first in range(0, span, chunk) for h in range(heads)]
    groups = in_pairs(list(range(blocks)))

    def scores(item):
        first, h = item
        q = q_ref[index, first : first + chunk, h * group : (h + 1) * group].reshape(chunk * group, dim) * scale
        q6 = query_terms(q)
        limit = begin + first + 1 + lax.broadcasted_iota(jnp.int32, (1, chunk * group), 1) // group
        return [
            functools.partial(
                lambda g: [score_block(keys[h][b], q6, limit, at_pos[b]) for b in g], g
            )
            for g in groups
        ]

    steps = [(n, g, make) for n, item in enumerate(items) for g, make in zip(groups, scores(item))]
    ahead = steps[0][2]()
    state = None
    copies = []
    for at, (n, g, _) in enumerate(steps):
        now, ahead = ahead, steps[at + 1][2]() if at + 1 < len(steps) else None
        first, h = items[n]
        cols = pl.ds(first * group, chunk * group)
        if g is groups[0]:
            state = get_state(*state_in, h, cols) if started else None
        state = fold(state, now, [vals[h][b] for b in g])
        if g is not groups[-1]:
            continue
        if not finish:
            put_state(state, outs[0], outs[1], h, cols)
            continue
        out_ref, hold, sems = outs[0], outs[-2], outs[-1]
        hold[n] = (state[2] * (1.0 / state[1])).T.reshape(chunk, group, dim)
        copy = pltpu.make_async_copy(
            hold.at[n], out_ref.at[index, pl.ds(first, chunk), pl.ds(h * group, group)], sems.at[n]
        )
        copy.start()
        copies.append(copy)
    if finish:
        outs[1][...] = jnp.zeros_like(outs[1])
    for copy in copies:
        copy.wait()


CHUNK = 64
SMEM_SPEC = pl.BlockSpec(memory_space=pltpu.SMEM)
VMEM_SPEC = pl.BlockSpec(memory_space=pltpu.VMEM)
ANY_SPEC = pl.BlockSpec(memory_space=pl.ANY)


def prefill_request(index, lengths, prefill_q, kv_list, first_block, heads, scale, state=None, finish=True, carried=None, after=()):
    nreq, span, q_heads, dim = prefill_q.shape
    group = q_heads // heads
    blocks = len(kv_list)
    started = state is not None
    state = list(state) if started else []
    unread = list(after) + ([carried] if carried is not None else [])
    alias = {2 + blocks + len(state) + len(after): 0} if carried is not None else {}
    keys = sum(kv.shape[2] for kv in kv_list) // heads
    scratch = []
    if finish:
        out_specs = [ANY_SPEC, VMEM_SPEC]
        out_shape = [jax.ShapeDtypeStruct(prefill_q.shape, F32), jax.ShapeDtypeStruct((8, 128), F32)]
        chunk = min(span, CHUNK)
        items = span // chunk * heads
        scratch = [pltpu.VMEM((items, chunk, group, dim), F32), pltpu.SemaphoreType.DMA((items,))]
    else:
        out_specs = [VMEM_SPEC, VMEM_SPEC]
        out_shape = state_shapes(heads, dim, span * group)
    return pl.pallas_call(
        functools.partial(prefill_kernel, (index, blocks, first_block, started, finish, len(unread)), heads, scale),
        in_specs=[SMEM_SPEC] + [VMEM_SPEC] * (1 + blocks + len(state)) + [ANY_SPEC] * len(unread),
        out_specs=out_specs,
        out_shape=out_shape,
        scratch_shapes=scratch,
        input_output_aliases=alias,
        compiler_params=pltpu.CompilerParams(vmem_limit_bytes=16 * 2**20),
        cost_estimate=pl.CostEstimate(
            flops=span * q_heads * keys * dim,
            bytes_accessed=4 * (2 * span * q_heads * dim + 2 * heads * keys * dim),
            transcendentals=span * q_heads * keys,
        ),
        name="prefill",
    )(lengths, prefill_q, *kv_list, *state, *unread)


def decode_kernel(plan, heads, group, steps, scale, *refs):
    index, near, blocks, first_block, started, finish, ready, unread = plan
    near_refs, far_ref, refs = refs[:near], refs[near], refs[near + 1 :]
    kv_refs, refs = refs[:blocks], refs[blocks:]
    state_in = refs[:2] if started else None
    refs = refs[2 if started else 0 :]
    ready_refs, outs = refs[:ready], refs[ready + unread :]
    side = lax.rem(lax.axis_index("head"), 2)
    at_pos = block_starts(blocks, first_block, kv_refs[0].shape[2] // heads)
    _, nreq, per, _, dim = far_ref.shape
    q_rows = steps * heads * group
    rows = steps * group
    slots = [(ref, side, n) for ref in near_refs for n in range(per)]
    slots += [(far_ref, j, n) for j in range(near) for n in range(per)]
    every = pl.ds(0, len(slots) * rows)
    at_limit = q_rows + 2 * heads * steps
    lane = lax.broadcasted_iota(jnp.int32, (1, len(slots) * rows), 1)
    limit = jnp.zeros(lane.shape, F32)
    for i, (ref, lead, n) in enumerate(slots):
        wide = jnp.broadcast_to(ref[lead, index, n, at_limit : at_limit + 1, 0:1], lane.shape)
        limit = jnp.where(lane // rows == i, wide, limit)
    limit = limit.astype(jnp.int32)
    if finish:
        for i in range(ready):
            first = i // 2
            outs[i % 2][:, first : first + 1] = ready_refs[i][...]
    for head in range(heads):
        own = slice(head * group, (head + 1) * group)
        q = jnp.concatenate(
            [
                ref[lead, index, n, 0:q_rows].reshape(steps, heads * group, dim)[:, own].reshape(rows, dim)
                for ref, lead, n in slots
            ],
            axis=0,
        )
        q6 = query_terms(q * scale)
        state = get_state(*state_in, head, every) if started else None
        for g, group_blocks in enumerate(in_pairs(list(range(blocks)))):
            parts = [
                score_block(key_terms(cache_head(kv_refs[b], 0, head, heads)), q6, limit, at_pos[b])
                for b in group_blocks
            ]
            vals = [value_terms(cache_head(kv_refs[b], 1, head, heads)) for b in group_blocks]
            if g == 0 and not started:
                drafts = [
                    jnp.concatenate(
                        [
                            ref[lead, index, n, pl.ds(q_rows + which * heads + head, steps, stride=2 * heads), :]
                            for ref, lead, n in slots
                        ],
                        axis=0,
                    )
                    for which in range(2)
                ]
                s = lax.dot_general(
                    key_terms(drafts[0]), q6, (((1,), (1,)), ((), ())), preferred_element_type=F32
                )
                key = lax.broadcasted_iota(jnp.int32, s.shape, 0)
                row = lax.broadcasted_iota(jnp.int32, s.shape, 1)
                seen = (row // rows == key // steps) & (key % steps <= row % rows // group)
                parts.append(jnp.where(seen, s, NEG_FILL))
                vals.append(value_terms(drafts[1]))
            state = fold(state, parts, vals)
        if not finish:
            put_state(state, outs[0], outs[1], head, every)
            continue
        out = (state[2] * (1.0 / state[1])).T
        for i in range(len(slots)):
            dst, j, n = outs[i // (near * per)], i // per % near, i % per
            for step in range(steps):
                first = step * heads * group + head * group
                at = i * rows + step * group
                dst[j, dst.shape[1] - 1, n, first : first + group] = out[at : at + group]


def decode_request(
    index, near, far, kv_list, first_block, heads, group, steps, scale, state=None, finish=True, ready=(), after=()
):
    count, _, per, packet_rows, dim = far.shape
    blocks = len(kv_list)
    q_rows = steps * heads * group
    all_rows = 2 * count * per * steps * group
    started = state is not None
    state = list(state) if started else []
    ready_flat = [a for one in ready for a in one]
    if finish:
        out_shape = [jax.ShapeDtypeStruct((count, len(ready) + 1, per, q_rows, dim), F32)] * 2
    else:
        out_shape = state_shapes(heads, dim, all_rows)
    keys = sum(kv.shape[2] for kv in kv_list) // heads
    plan = (index, count, blocks, first_block, started, finish, len(ready_flat), len(after))
    operands = count + 1 + blocks + len(state) + len(ready_flat)
    return pl.pallas_call(
        functools.partial(decode_kernel, plan, heads, group, steps, scale),
        in_specs=[VMEM_SPEC] * operands + [ANY_SPEC] * len(after),
        out_specs=[VMEM_SPEC] * len(out_shape),
        out_shape=out_shape,
        compiler_params=pltpu.CompilerParams(vmem_limit_bytes=12 * 2**20),
        cost_estimate=pl.CostEstimate(
            flops=all_rows * heads * keys * dim,
            bytes_accessed=4 * (4 * count * per * packet_rows * dim + 2 * heads * keys * dim),
            transcendentals=all_rows * heads * keys,
        ),
        name="decode",
    )(*near, far, *kv_list, *state, *ready_flat, *after)


def take_kernel(index, src, dst, sem):
    copy = pltpu.make_async_copy(src.at[pl.ds(index, 1)], dst, sem)
    copy.start()
    copy.wait()


def take(index, array):
    return pl.pallas_call(
        functools.partial(take_kernel, index),
        in_specs=[pl.BlockSpec(memory_space=pltpu.HBM)],
        out_specs=VMEM_SPEC,
        out_shape=jax.ShapeDtypeStruct((1,) + array.shape[1:], array.dtype),
        scratch_shapes=[pltpu.SemaphoreType.DMA],
        compiler_params=pltpu.CompilerParams(vmem_limit_bytes=4 * 2**20),
        name="take",
    )(array)


def pack_kernel(unread, lengths, q_ref, kv_ref, *refs):
    outs = refs[unread:]
    half = len(outs)
    _, nreq, per, rows, dim = outs[0].shape
    q_rows, kv_rows = q_ref.shape[2], kv_ref.shape[2]
    for j, out in enumerate(outs):
        pair = pair_of(lax.axis_index("rep"), j, half)
        for c in range(2):
            for i in range(nreq):
                request = (pair * 2 + c) * nreq + i
                for n in range(per):
                    out[c, i, n, 0:q_rows] = q_ref[request, n]
                    out[c, i, n, q_rows : q_rows + kv_rows] = kv_ref[request, n]
                    reads = jnp.full((rows - q_rows - kv_rows, dim), lengths[request, n], jnp.int32)
                    out[c, i, n, q_rows + kv_rows :] = reads.astype(F32)


def pack(lengths, q, kv, half, nreq, after):
    requests, per, q_rows, dim = q.shape
    shape = jax.ShapeDtypeStruct((2, nreq, per, q_rows + kv.shape[2] + 8, dim), F32)
    return pl.pallas_call(
        functools.partial(pack_kernel, len(after)),
        in_specs=[SMEM_SPEC, VMEM_SPEC, VMEM_SPEC] + [ANY_SPEC] * len(after),
        out_specs=[VMEM_SPEC] * half,
        out_shape=[shape] * half,
        compiler_params=pltpu.CompilerParams(vmem_limit_bytes=4 * 2**20),
        cost_estimate=pl.CostEstimate(flops=10**11, bytes_accessed=10**6, transcendentals=0),
        name="pack",
    )(lengths, q, kv, *after)


def other_kernel(count, *refs):
    out = refs[-1]
    for j, ref in enumerate(refs[:count]):
        out[j] = ref[1 - lax.rem(lax.axis_index("head"), 2)]


def other_side(near, after):
    return pl.pallas_call(
        functools.partial(other_kernel, len(near)),
        in_specs=[VMEM_SPEC] * len(near) + [ANY_SPEC] * len(after),
        out_specs=VMEM_SPEC,
        out_shape=jax.ShapeDtypeStruct((len(near),) + near[0].shape[1:], F32),
        compiler_params=pltpu.CompilerParams(vmem_limit_bytes=4 * 2**20),
        name="other_side",
    )(*near, *after)


def join_kernel(kept, back, *outs):
    side = lax.rem(lax.axis_index("head"), 2)
    for j, out in enumerate(outs):
        out[side] = kept[j]
        out[1 - side] = back[j]


def join(kept, back):
    count = kept.shape[0]
    return pl.pallas_call(
        join_kernel,
        in_specs=[VMEM_SPEC] * 2,
        out_specs=[VMEM_SPEC] * count,
        out_shape=[jax.ShapeDtypeStruct((2,) + kept.shape[1:], F32)] * count,
        compiler_params=pltpu.CompilerParams(vmem_limit_bytes=4 * 2**20),
        name="join",
    )(kept, back)


def place_kernel(*refs):
    o_ref, count = refs[-1], len(refs) - 1
    size = refs[0].shape[0]
    for j in range(count):
        o_ref[pl.ds(pair_of(lax.axis_index("rep"), j, count) * size, size)] = refs[j][...]


def place(pieces):
    size, per, rows, dim = pieces[0].shape
    count = len(pieces)
    return pl.pallas_call(
        place_kernel,
        in_specs=[VMEM_SPEC] * count,
        out_specs=VMEM_SPEC,
        out_shape=jax.ShapeDtypeStruct((count * size, per, rows, dim), F32),
        compiler_params=pltpu.CompilerParams(vmem_limit_bytes=4 * 2**20),
        name="place",
    )(*pieces)


def on_device(kv_cache, prefill_q, decode_q, decode_kv, lengths, row_length):
    ctx_count, head_count, rep_count = lax.axis_size("ctx"), lax.axis_size("head"), lax.axis_size("rep")
    nreq, _, block_len, heads, dim = kv_cache.shape
    group = prefill_q.shape[2] // heads
    requests, per, steps, q_heads, _ = decode_q.shape
    scale = LOG2E / math.sqrt(dim)
    half = head_count // 2

    flat = kv_cache.reshape(nreq, 2, block_len * heads, dim)
    own = [take(i, flat) for i in range(nreq)]
    held = [[own[i]] for i in range(nreq)]
    for shift in range(1, ctx_count):
        perm = [((i + shift) % ctx_count, i) for i in range(ctx_count)]
        for i in range(nreq):
            held[i].append(lax.ppermute(own[i], "ctx", perm))

    routes = [
        [
            (s * rep_count + t, (pair_of(t, j, half) * 2 + core_of(t, half)) * rep_count + s)
            for s in range(head_count)
            for t in range(rep_count)
        ]
        for j in range(half)
    ]
    swap = [(i, i ^ 1) for i in range(head_count)]
    packets = pack(
        row_length,
        decode_q.reshape(requests, per, steps * q_heads, dim),
        decode_kv.reshape(requests, per, steps * 2 * heads, dim),
        half,
        nreq,
        own,
    )
    near = [lax.ppermute(packets[j], ("head", "rep"), routes[j]) for j in range(half)]
    last = nreq - 1
    prefill_state = prefill_request(last, lengths, prefill_q, held[last][:1], 0, heads, scale, finish=False, after=packets[:1])
    prefill_out, token = None, prefill_state[1]
    for i in range(last):
        prefill_out, token = prefill_request(i, lengths, prefill_q, held[i], 0, heads, scale, carried=prefill_out, after=(token,))
    far = lax.ppermute(other_side(near, (token,)), "head", swap)
    ready = [decode_request(i, near, far, held[i], 0, heads, group, steps, scale) for i in range(last)]
    kept, sent = decode_request(
        last, near, far, held[last], 0, heads, group, steps, scale, ready=ready, after=(prefill_state[0],)
    )
    prefill_out, _ = prefill_request(
        last, lengths, prefill_q, held[last][1:], 1, heads, scale, state=prefill_state, carried=prefill_out
    )
    joined = join(kept, lax.ppermute(sent, "head", swap))
    homes = [lax.ppermute(joined[j], ("head", "rep"), [(b, a) for a, b in routes[j]]) for j in range(half)]
    decode_out = place([a.reshape((2 * nreq,) + a.shape[2:]) for a in homes]).reshape(decode_q.shape)
    return (prefill_out, decode_out)


def solution(mesh):
    in_specs = (
        P("head", None, "ctx", "rep", None),
        P("head", "ctx", "rep", None),
        P(None, ("ctx", "rep"), None, "head", None),
        P(None, ("ctx", "rep"), None, None, "head", None),
        P(),
        P(None, ("ctx", "rep")),
    )
    out_specs = (P("head", "ctx", "rep", None), P(None, ("ctx", "rep"), None, "head", None))
    return jax.shard_map(on_device, mesh=mesh, in_specs=in_specs, out_specs=out_specs, check_vma=False)
```

```python
import functools
import math

import jax
import jax.numpy as jnp
from jax import lax
from jax.experimental import pallas as pl
from jax.experimental.pallas import tpu as pltpu
from jax.sharding import PartitionSpec as P

NEG_FILL = -1e30
LOG2E = math.log2(math.e)
F32 = jnp.float32
BF16 = jnp.bfloat16


def split_two(x):
    high = x.astype(BF16)
    return high, (x - high.astype(F32)).astype(BF16)


def split_three(x):
    high = x.astype(BF16)
    rest = x - high.astype(F32)
    mid = rest.astype(BF16)
    return high, mid, (rest - mid.astype(F32)).astype(BF16)


def query_terms(q):
    a, b, c = split_three(q)
    return jnp.concatenate([a, b, a, b, a, c], axis=-1)


def key_terms(k):
    a, b, c = split_three(k)
    return jnp.concatenate([a, a, b, b, c, a], axis=-1)


def value_terms(v):
    return jnp.concatenate(split_two(v.T), axis=0)


def score_block(k6, q6, limit, first_pos):
    s = lax.dot_general(k6, q6, (((1,), (1,)), ((), ())), preferred_element_type=F32)
    return jnp.where(lax.broadcasted_iota(jnp.int32, s.shape, 0) < limit - first_pos, s, NEG_FILL)


def weighted(vv, p):
    dim = vv.shape[0] // 2
    a, b = split_two(p)
    both = jnp.dot(vv, a, preferred_element_type=F32)
    return (both[:dim] + both[dim:]) + jnp.dot(vv[:dim], b, preferred_element_type=F32)


def fold(state, scores, values):
    top = functools.reduce(jnp.maximum, [jnp.max(s, axis=0, keepdims=True) for s in scores])
    if state is not None:
        top = jnp.maximum(top, state[0])
    weights = [jnp.exp2(s - top) for s in scores]
    total = functools.reduce(jnp.add, [jnp.sum(w, axis=0, keepdims=True) for w in weights])
    acc = functools.reduce(jnp.add, [weighted(vv, w) for vv, w in zip(values, weights)])
    if state is not None:
        factor = jnp.exp2(state[0] - top)
        total = total + state[1] * factor
        acc = acc + state[2] * factor
    return top, total, acc


def in_pairs(blocks):
    return [blocks[i : i + 2] for i in range(0, len(blocks), 2)]


def cache_head(ref, which, head, heads):
    return ref[0, which, pl.ds(head, ref.shape[2] // heads, stride=heads), :]


def put_state(state, acc_ref, stat_ref, head, cols):
    acc_ref[head, :, cols] = state[2]
    stat_ref[head, 0:1, cols] = state[0]
    stat_ref[head, 1:2, cols] = state[1]


def get_state(acc_ref, stat_ref, head, cols):
    return stat_ref[head, 0:1, cols], stat_ref[head, 1:2, cols], acc_ref[head, :, cols]


def state_shapes(heads, dim, rows):
    return [jax.ShapeDtypeStruct((heads, dim, rows), F32), jax.ShapeDtypeStruct((heads, 8, rows), F32)]


def pair_of(s, t, j, half):
    return (t // 2 + j + 1 + core_of(t) + s // half + s % 2) % half


def core_of(t):
    return (t + t // 2) % 2


def block_starts(count, first, block_len):
    here, total = lax.axis_index("ctx"), lax.axis_size("ctx")
    return [lax.rem(here + (first + b), total) * block_len for b in range(count)]


def prefill_kernel(plan, heads, scale, lengths, q_ref, *refs):
    index, blocks, first_block, started, finish, unread = plan
    kv_refs, refs = refs[:blocks], refs[blocks:]
    state_in = refs[:2] if started else None
    outs = refs[(2 if started else 0) + unread :]
    _, span, q_heads, dim = q_ref.shape
    group = q_heads // heads
    chunk = min(span, CHUNK)
    total = lax.axis_size("ctx") * span
    begin = lengths[lax.axis_index("head") * q_ref.shape[0] + index] - total + lax.axis_index("ctx") * span
    at_pos = block_starts(blocks, first_block, kv_refs[0].shape[2] // heads)
    keys = [[key_terms(cache_head(ref, 0, h, heads)) for ref in kv_refs] for h in range(heads)]
    vals = [[value_terms(cache_head(ref, 1, h, heads)) for ref in kv_refs] for h in range(heads)]
    items = [(first, h) for first in range(0, span, chunk) for h in range(heads)]
    groups = in_pairs(list(range(blocks)))

    def scores(item):
        first, h = item
        q = q_ref[index, first : first + chunk, h * group : (h + 1) * group].reshape(chunk * group, dim) * scale
        q6 = query_terms(q)
        limit = begin + first + 1 + lax.broadcasted_iota(jnp.int32, (1, chunk * group), 1) // group
        return [
            functools.partial(
                lambda g: [score_block(keys[h][b], q6, limit, at_pos[b]) for b in g], g
            )
            for g in groups
        ]

    steps = [(n, g, make) for n, item in enumerate(items) for g, make in zip(groups, scores(item))]
    ahead = steps[0][2]()
    state = None
    copies = []
    for at, (n, g, _) in enumerate(steps):
        now, ahead = ahead, steps[at + 1][2]() if at + 1 < len(steps) else None
        first, h = items[n]
        cols = pl.ds(first * group, chunk * group)
        if g is groups[0]:
            state = get_state(*state_in, h, cols) if started else None
        state = fold(state, now, [vals[h][b] for b in g])
        if g is not groups[-1]:
            continue
        if not finish:
            put_state(state, outs[0], outs[1], h, cols)
            continue
        out_ref, hold, sems = outs[0], outs[-2], outs[-1]
        hold[n] = (state[2] * (1.0 / state[1])).T.reshape(chunk, group, dim)
        copy = pltpu.make_async_copy(
            hold.at[n], out_ref.at[index, pl.ds(first, chunk), pl.ds(h * group, group)], sems.at[n]
        )
        copy.start()
        copies.append(copy)
    if finish:
        outs[1][...] = jnp.zeros_like(outs[1])
    for copy in copies:
        copy.wait()


CHUNK = 64
SMEM_SPEC = pl.BlockSpec(memory_space=pltpu.SMEM)
VMEM_SPEC = pl.BlockSpec(memory_space=pltpu.VMEM)
ANY_SPEC = pl.BlockSpec(memory_space=pl.ANY)


def prefill_request(index, lengths, prefill_q, kv_list, first_block, heads, scale, state=None, finish=True, carried=None, after=()):
    nreq, span, q_heads, dim = prefill_q.shape
    group = q_heads // heads
    blocks = len(kv_list)
    started = state is not None
    state = list(state) if started else []
    unread = list(after) + ([carried] if carried is not None else [])
    alias = {2 + blocks + len(state) + len(after): 0} if carried is not None else {}
    keys = sum(kv.shape[2] for kv in kv_list) // heads
    scratch = []
    if finish:
        out_specs = [ANY_SPEC, VMEM_SPEC]
        out_shape = [jax.ShapeDtypeStruct(prefill_q.shape, F32), jax.ShapeDtypeStruct((8, 128), F32)]
        chunk = min(span, CHUNK)
        items = span // chunk * heads
        scratch = [pltpu.VMEM((items, chunk, group, dim), F32), pltpu.SemaphoreType.DMA((items,))]
    else:
        out_specs = [VMEM_SPEC, VMEM_SPEC]
        out_shape = state_shapes(heads, dim, span * group)
    return pl.pallas_call(
        functools.partial(prefill_kernel, (index, blocks, first_block, started, finish, len(unread)), heads, scale),
        in_specs=[SMEM_SPEC] + [VMEM_SPEC] * (1 + blocks + len(state)) + [ANY_SPEC] * len(unread),
        out_specs=out_specs,
        out_shape=out_shape,
        scratch_shapes=scratch,
        input_output_aliases=alias,
        compiler_params=pltpu.CompilerParams(vmem_limit_bytes=16 * 2**20),
        cost_estimate=pl.CostEstimate(
            flops=span * q_heads * keys * dim,
            bytes_accessed=4 * (2 * span * q_heads * dim + 2 * heads * keys * dim),
            transcendentals=span * q_heads * keys,
        ),
        name="prefill",
    )(lengths, prefill_q, *kv_list, *state, *unread)


def decode_kernel(plan, heads, group, steps, scale, *refs):
    index, near, blocks, first_block, started, finish, ready, unread = plan
    near_refs, far_ref, refs = refs[:near], refs[near], refs[near + 1 :]
    kv_refs, refs = refs[:blocks], refs[blocks:]
    state_in = refs[:2] if started else None
    refs = refs[2 if started else 0 :]
    ready_refs, outs = refs[:ready], refs[ready + unread :]
    side = lax.rem(lax.axis_index("head"), 2)
    at_pos = block_starts(blocks, first_block, kv_refs[0].shape[2] // heads)
    _, nreq, per, _, dim = far_ref.shape
    q_rows = steps * heads * group
    rows = steps * group
    slots = [(ref, side, n) for ref in near_refs for n in range(per)]
    slots += [(far_ref, j, n) for j in range(near) for n in range(per)]
    every = pl.ds(0, len(slots) * rows)
    at_limit = q_rows + 2 * heads * steps
    lane = lax.broadcasted_iota(jnp.int32, (1, len(slots) * rows), 1)
    limit = jnp.zeros(lane.shape, F32)
    for i, (ref, lead, n) in enumerate(slots):
        wide = jnp.broadcast_to(ref[lead, index, n, at_limit : at_limit + 1, 0:1], lane.shape)
        limit = jnp.where(lane // rows == i, wide, limit)
    limit = limit.astype(jnp.int32)
    if finish:
        for i in range(ready):
            first = i // 2
            outs[i % 2][:, first : first + 1] = ready_refs[i][...]
    for head in range(heads):
        own = slice(head * group, (head + 1) * group)
        q = jnp.concatenate(
            [
                ref[lead, index, n, 0:q_rows].reshape(steps, heads * group, dim)[:, own].reshape(rows, dim)
                for ref, lead, n in slots
            ],
            axis=0,
        )
        q6 = query_terms(q * scale)
        state = get_state(*state_in, head, every) if started else None
        for g, group_blocks in enumerate(in_pairs(list(range(blocks)))):
            parts = [
                score_block(key_terms(cache_head(kv_refs[b], 0, head, heads)), q6, limit, at_pos[b])
                for b in group_blocks
            ]
            vals = [value_terms(cache_head(kv_refs[b], 1, head, heads)) for b in group_blocks]
            if g == 0 and not started:
                drafts = [
                    jnp.concatenate(
                        [
                            ref[lead, index, n, pl.ds(q_rows + which * heads + head, steps, stride=2 * heads), :]
                            for ref, lead, n in slots
                        ],
                        axis=0,
                    )
                    for which in range(2)
                ]
                s = lax.dot_general(
                    key_terms(drafts[0]), q6, (((1,), (1,)), ((), ())), preferred_element_type=F32
                )
                key = lax.broadcasted_iota(jnp.int32, s.shape, 0)
                row = lax.broadcasted_iota(jnp.int32, s.shape, 1)
                seen = (row // rows == key // steps) & (key % steps <= row % rows // group)
                parts.append(jnp.where(seen, s, NEG_FILL))
                vals.append(value_terms(drafts[1]))
            state = fold(state, parts, vals)
        if not finish:
            put_state(state, outs[0], outs[1], head, every)
            continue
        out = (state[2] * (1.0 / state[1])).T
        for i in range(len(slots)):
            dst, j, n = outs[i // (near * per)], i // per % near, i % per
            for step in range(steps):
                first = step * heads * group + head * group
                at = i * rows + step * group
                dst[j, dst.shape[1] - 1, n, first : first + group] = out[at : at + group]


def decode_request(
    index, near, far, kv_list, first_block, heads, group, steps, scale, state=None, finish=True, ready=(), after=()
):
    count, _, per, packet_rows, dim = far.shape
    blocks = len(kv_list)
    q_rows = steps * heads * group
    all_rows = 2 * count * per * steps * group
    started = state is not None
    state = list(state) if started else []
    ready_flat = [a for one in ready for a in one]
    if finish:
        out_shape = [jax.ShapeDtypeStruct((count, len(ready) + 1, per, q_rows, dim), F32)] * 2
    else:
        out_shape = state_shapes(heads, dim, all_rows)
    keys = sum(kv.shape[2] for kv in kv_list) // heads
    plan = (index, count, blocks, first_block, started, finish, len(ready_flat), len(after))
    operands = count + 1 + blocks + len(state) + len(ready_flat)
    return pl.pallas_call(
        functools.partial(decode_kernel, plan, heads, group, steps, scale),
        in_specs=[VMEM_SPEC] * operands + [ANY_SPEC] * len(after),
        out_specs=[VMEM_SPEC] * len(out_shape),
        out_shape=out_shape,
        compiler_params=pltpu.CompilerParams(vmem_limit_bytes=12 * 2**20),
        cost_estimate=pl.CostEstimate(
            flops=all_rows * heads * keys * dim,
            bytes_accessed=4 * (4 * count * per * packet_rows * dim + 2 * heads * keys * dim),
            transcendentals=all_rows * heads * keys,
        ),
        name="decode",
    )(*near, far, *kv_list, *state, *ready_flat, *after)


def take_kernel(index, src, dst, sem):
    copy = pltpu.make_async_copy(src.at[pl.ds(index, 1)], dst, sem)
    copy.start()
    copy.wait()


def take(index, array):
    return pl.pallas_call(
        functools.partial(take_kernel, index),
        in_specs=[pl.BlockSpec(memory_space=pltpu.HBM)],
        out_specs=VMEM_SPEC,
        out_shape=jax.ShapeDtypeStruct((1,) + array.shape[1:], array.dtype),
        scratch_shapes=[pltpu.SemaphoreType.DMA],
        compiler_params=pltpu.CompilerParams(vmem_limit_bytes=4 * 2**20),
        name="take",
    )(array)


def pack_kernel(unread, lengths, q_ref, kv_ref, *refs):
    outs = refs[unread:]
    half = len(outs)
    _, nreq, per, rows, dim = outs[0].shape
    q_rows, kv_rows = q_ref.shape[2], kv_ref.shape[2]
    for j, out in enumerate(outs):
        pair = pair_of(lax.axis_index("head"), lax.axis_index("rep"), j, half)
        for c in range(2):
            for i in range(nreq):
                request = (pair * 2 + c) * nreq + i
                for n in range(per):
                    out[c, i, n, 0:q_rows] = q_ref[request, n]
                    out[c, i, n, q_rows : q_rows + kv_rows] = kv_ref[request, n]
                    reads = jnp.full((rows - q_rows - kv_rows, dim), lengths[request, n], jnp.int32)
                    out[c, i, n, q_rows + kv_rows :] = reads.astype(F32)


def pack(lengths, q, kv, half, nreq, after):
    requests, per, q_rows, dim = q.shape
    shape = jax.ShapeDtypeStruct((2, nreq, per, q_rows + kv.shape[2] + 8, dim), F32)
    return pl.pallas_call(
        functools.partial(pack_kernel, len(after)),
        in_specs=[SMEM_SPEC, VMEM_SPEC, VMEM_SPEC] + [ANY_SPEC] * len(after),
        out_specs=[VMEM_SPEC] * half,
        out_shape=[shape] * half,
        compiler_params=pltpu.CompilerParams(vmem_limit_bytes=4 * 2**20),
        cost_estimate=pl.CostEstimate(flops=10**11, bytes_accessed=10**6, transcendentals=0),
        name="pack",
    )(lengths, q, kv, *after)


def other_kernel(count, *refs):
    out = refs[-1]
    for j, ref in enumerate(refs[:count]):
        out[j] = ref[1 - lax.rem(lax.axis_index("head"), 2)]


def other_side(near, after):
    return pl.pallas_call(
        functools.partial(other_kernel, len(near)),
        in_specs=[VMEM_SPEC] * len(near) + [ANY_SPEC] * len(after),
        out_specs=VMEM_SPEC,
        out_shape=jax.ShapeDtypeStruct((len(near),) + near[0].shape[1:], F32),
        compiler_params=pltpu.CompilerParams(vmem_limit_bytes=4 * 2**20),
        name="other_side",
    )(*near, *after)


def join_kernel(kept, back, *outs):
    side = lax.rem(lax.axis_index("head"), 2)
    for j, out in enumerate(outs):
        out[side] = kept[j]
        out[1 - side] = back[j]


def join(kept, back):
    count = kept.shape[0]
    return pl.pallas_call(
        join_kernel,
        in_specs=[VMEM_SPEC] * 2,
        out_specs=[VMEM_SPEC] * count,
        out_shape=[jax.ShapeDtypeStruct((2,) + kept.shape[1:], F32)] * count,
        compiler_params=pltpu.CompilerParams(vmem_limit_bytes=4 * 2**20),
        name="join",
    )(kept, back)


def place_kernel(*refs):
    o_ref, count = refs[-1], len(refs) - 1
    size = refs[0].shape[0]
    for j in range(count):
        o_ref[pl.ds(pair_of(lax.axis_index("head"), lax.axis_index("rep"), j, count) * size, size)] = refs[j][...]


def place(pieces):
    size, per, rows, dim = pieces[0].shape
    count = len(pieces)
    return pl.pallas_call(
        place_kernel,
        in_specs=[VMEM_SPEC] * count,
        out_specs=VMEM_SPEC,
        out_shape=jax.ShapeDtypeStruct((count * size, per, rows, dim), F32),
        compiler_params=pltpu.CompilerParams(vmem_limit_bytes=4 * 2**20),
        name="place",
    )(*pieces)


def on_device(kv_cache, prefill_q, decode_q, decode_kv, lengths, row_length):
    ctx_count, head_count, rep_count = lax.axis_size("ctx"), lax.axis_size("head"), lax.axis_size("rep")
    nreq, _, block_len, heads, dim = kv_cache.shape
    group = prefill_q.shape[2] // heads
    requests, per, steps, q_heads, _ = decode_q.shape
    scale = LOG2E / math.sqrt(dim)
    half = head_count // 2

    flat = kv_cache.reshape(nreq, 2, block_len * heads, dim)
    own = [take(i, flat) for i in range(nreq)]
    held = [[own[i]] for i in range(nreq)]
    for shift in range(1, ctx_count):
        perm = [((i + shift) % ctx_count, i) for i in range(ctx_count)]
        for i in range(nreq):
            held[i].append(lax.ppermute(own[i], "ctx", perm))

    routes = [
        [
            (s * rep_count + t, (pair_of(s, t, j, half) * 2 + core_of(t)) * rep_count + s)
            for s in range(head_count)
            for t in range(rep_count)
        ]
        for j in range(half)
    ]
    swap = [(i, i ^ 1) for i in range(head_count)]
    packets = pack(
        row_length,
        decode_q.reshape(requests, per, steps * q_heads, dim),
        decode_kv.reshape(requests, per, steps * 2 * heads, dim),
        half,
        nreq,
        own,
    )
    near = [lax.ppermute(packets[j], ("head", "rep"), routes[j]) for j in range(half)]
    last = nreq - 1
    prefill_state = prefill_request(last, lengths, prefill_q, held[last][:1], 0, heads, scale, finish=False, after=packets[:1])
    prefill_out, token = None, prefill_state[1]
    for i in range(last):
        prefill_out, token = prefill_request(i, lengths, prefill_q, held[i], 0, heads, scale, carried=prefill_out, after=(token,))
    far = lax.ppermute(other_side(near, (token,)), "head", swap)
    ready = [decode_request(i, near, far, held[i], 0, heads, group, steps, scale) for i in range(last)]
    decode_state = decode_request(
        last, near, far, held[last][:1], 0, heads, group, steps, scale, finish=False, after=ready[-1][:1]
    )
    kept, sent = decode_request(
        last, near, far, held[last][1:], 1, heads, group, steps, scale, state=decode_state, ready=ready
    )
    prefill_out, _ = prefill_request(
        last, lengths, prefill_q, held[last][1:], 1, heads, scale, state=prefill_state, carried=prefill_out
    )
    joined = join(kept, lax.ppermute(sent, "head", swap))
    homes = [lax.ppermute(joined[j], ("head", "rep"), [(b, a) for a, b in routes[j]]) for j in range(half)]
    decode_out = place([a.reshape((2 * nreq,) + a.shape[2:]) for a in homes]).reshape(decode_q.shape)
    return (prefill_out, decode_out)


def solution(mesh):
    in_specs = (
        P("head", None, "ctx", "rep", None),
        P("head", "ctx", "rep", None),
        P(None, ("ctx", "rep"), None, "head", None),
        P(None, ("ctx", "rep"), None, None, "head", None),
        P(),
        P(None, ("ctx", "rep")),
    )
    out_specs = (P("head", "ctx", "rep", None), P(None, ("ctx", "rep"), None, "head", None))
    return jax.shard_map(on_device, mesh=mesh, in_specs=in_specs, out_specs=out_specs, check_vma=False)
```

```python
import functools
import math

import jax
import jax.numpy as jnp
from jax import lax
from jax.experimental import pallas as pl
from jax.experimental.pallas import tpu as pltpu
from jax.sharding import PartitionSpec as P

NEG_FILL = -1e30
LOG2E = math.log2(math.e)
F32 = jnp.float32
BF16 = jnp.bfloat16


def split_two(x):
    high = x.astype(BF16)
    return high, (x - high.astype(F32)).astype(BF16)


def split_three(x):
    high = x.astype(BF16)
    rest = x - high.astype(F32)
    mid = rest.astype(BF16)
    return high, mid, (rest - mid.astype(F32)).astype(BF16)


def query_terms(q):
    a, b, c = split_three(q)
    return jnp.concatenate([a, b, a, b, a, c], axis=-1)


def key_terms(k):
    a, b, c = split_three(k)
    return jnp.concatenate([a, a, b, b, c, a], axis=-1)


def value_terms(v):
    return jnp.concatenate(split_two(v.T), axis=0)


def score_block(k6, q6, limit, first_pos):
    s = lax.dot_general(k6, q6, (((1,), (1,)), ((), ())), preferred_element_type=F32)
    return jnp.where(lax.broadcasted_iota(jnp.int32, s.shape, 0) < limit - first_pos, s, NEG_FILL)


def weighted(vv, p):
    dim = vv.shape[0] // 2
    a, b = split_two(p)
    both = jnp.dot(vv, a, preferred_element_type=F32)
    return (both[:dim] + both[dim:]) + jnp.dot(vv[:dim], b, preferred_element_type=F32)


def fold(state, scores, values):
    top = functools.reduce(jnp.maximum, [jnp.max(s, axis=0, keepdims=True) for s in scores])
    if state is not None:
        top = jnp.maximum(top, state[0])
    weights = [jnp.exp2(s - top) for s in scores]
    total = functools.reduce(jnp.add, [jnp.sum(w, axis=0, keepdims=True) for w in weights])
    acc = functools.reduce(jnp.add, [weighted(vv, w) for vv, w in zip(values, weights)])
    if state is not None:
        factor = jnp.exp2(state[0] - top)
        total = total + state[1] * factor
        acc = acc + state[2] * factor
    return top, total, acc


def in_pairs(blocks):
    return [blocks[i : i + 2] for i in range(0, len(blocks), 2)]


def cache_head(ref, which, head, heads):
    return ref[0, which, pl.ds(head, ref.shape[2] // heads, stride=heads), :]


def put_state(state, acc_ref, stat_ref, head, cols):
    acc_ref[head, :, cols] = state[2]
    stat_ref[head, 0:1, cols] = state[0]
    stat_ref[head, 1:2, cols] = state[1]


def get_state(acc_ref, stat_ref, head, cols):
    return stat_ref[head, 0:1, cols], stat_ref[head, 1:2, cols], acc_ref[head, :, cols]


def state_shapes(heads, dim, rows):
    return [jax.ShapeDtypeStruct((heads, dim, rows), F32), jax.ShapeDtypeStruct((heads, 8, rows), F32)]


def pair_of(s, t, j, half):
    return (t // 2 + j + 1 + core_of(t) + s // half + s % 2) % half


def core_of(t):
    return (t + t // 2) % 2


def block_starts(count, first, block_len):
    here, total = lax.axis_index("ctx"), lax.axis_size("ctx")
    return [lax.rem(here + (first + b), total) * block_len for b in range(count)]


def prefill_kernel(plan, heads, scale, lengths, q_ref, *refs):
    index, blocks, first_block, started, finish, unread = plan
    kv_refs, refs = refs[:blocks], refs[blocks:]
    state_in = refs[:2] if started else None
    outs = refs[(2 if started else 0) + unread :]
    _, span, q_heads, dim = q_ref.shape
    group = q_heads // heads
    chunk = min(span, CHUNK)
    total = lax.axis_size("ctx") * span
    begin = lengths[lax.axis_index("head") * q_ref.shape[0] + index] - total + lax.axis_index("ctx") * span
    at_pos = block_starts(blocks, first_block, kv_refs[0].shape[2] // heads)
    keys = [[key_terms(cache_head(ref, 0, h, heads)) for ref in kv_refs] for h in range(heads)]
    vals = [[value_terms(cache_head(ref, 1, h, heads)) for ref in kv_refs] for h in range(heads)]
    items = [(first, h) for first in range(0, span, chunk) for h in range(heads)]
    groups = in_pairs(list(range(blocks)))

    def scores(item):
        first, h = item
        q = q_ref[index, first : first + chunk, h * group : (h + 1) * group].reshape(chunk * group, dim) * scale
        q6 = query_terms(q)
        limit = begin + first + 1 + lax.broadcasted_iota(jnp.int32, (1, chunk * group), 1) // group
        return [
            functools.partial(
                lambda g: [score_block(keys[h][b], q6, limit, at_pos[b]) for b in g], g
            )
            for g in groups
        ]

    steps = [(n, g, make) for n, item in enumerate(items) for g, make in zip(groups, scores(item))]
    ahead = steps[0][2]()
    state = None
    copies = []
    for at, (n, g, _) in enumerate(steps):
        now, ahead = ahead, steps[at + 1][2]() if at + 1 < len(steps) else None
        first, h = items[n]
        cols = pl.ds(first * group, chunk * group)
        if g is groups[0]:
            state = get_state(*state_in, h, cols) if started else None
        state = fold(state, now, [vals[h][b] for b in g])
        if g is not groups[-1]:
            continue
        if not finish:
            put_state(state, outs[0], outs[1], h, cols)
            continue
        out_ref, hold, sems = outs[0], outs[-2], outs[-1]
        hold[n] = (state[2] * (1.0 / state[1])).T.reshape(chunk, group, dim)
        copy = pltpu.make_async_copy(
            hold.at[n], out_ref.at[index, pl.ds(first, chunk), pl.ds(h * group, group)], sems.at[n]
        )
        copy.start()
        copies.append(copy)
    if finish:
        outs[1][...] = jnp.zeros_like(outs[1])
    for copy in copies:
        copy.wait()


CHUNK = 64
SMEM_SPEC = pl.BlockSpec(memory_space=pltpu.SMEM)
VMEM_SPEC = pl.BlockSpec(memory_space=pltpu.VMEM)
ANY_SPEC = pl.BlockSpec(memory_space=pl.ANY)


def prefill_request(index, lengths, prefill_q, kv_list, first_block, heads, scale, state=None, finish=True, carried=None, after=()):
    nreq, span, q_heads, dim = prefill_q.shape
    group = q_heads // heads
    blocks = len(kv_list)
    started = state is not None
    state = list(state) if started else []
    unread = list(after) + ([carried] if carried is not None else [])
    alias = {2 + blocks + len(state) + len(after): 0} if carried is not None else {}
    keys = sum(kv.shape[2] for kv in kv_list) // heads
    scratch = []
    if finish:
        out_specs = [ANY_SPEC, VMEM_SPEC]
        out_shape = [jax.ShapeDtypeStruct(prefill_q.shape, F32), jax.ShapeDtypeStruct((8, 128), F32)]
        chunk = min(span, CHUNK)
        items = span // chunk * heads
        scratch = [pltpu.VMEM((items, chunk, group, dim), F32), pltpu.SemaphoreType.DMA((items,))]
    else:
        out_specs = [VMEM_SPEC, VMEM_SPEC]
        out_shape = state_shapes(heads, dim, span * group)
    return pl.pallas_call(
        functools.partial(prefill_kernel, (index, blocks, first_block, started, finish, len(unread)), heads, scale),
        in_specs=[SMEM_SPEC] + [VMEM_SPEC] * (1 + blocks + len(state)) + [ANY_SPEC] * len(unread),
        out_specs=out_specs,
        out_shape=out_shape,
        scratch_shapes=scratch,
        input_output_aliases=alias,
        compiler_params=pltpu.CompilerParams(vmem_limit_bytes=16 * 2**20),
        cost_estimate=pl.CostEstimate(
            flops=span * q_heads * keys * dim,
            bytes_accessed=4 * (2 * span * q_heads * dim + 2 * heads * keys * dim),
            transcendentals=span * q_heads * keys,
        ),
        name="prefill",
    )(lengths, prefill_q, *kv_list, *state, *unread)


def decode_kernel(plan, heads, group, steps, scale, *refs):
    index, nreq, per, near, blocks, first_block, started, finish, ready, unread = plan
    near_refs, far_ref, refs = refs[:near], refs[near], refs[near + 1 :]
    kv_refs, refs = refs[:blocks], refs[blocks:]
    state_in = refs[:2] if started else None
    refs = refs[2 if started else 0 :]
    ready_refs, outs = refs[:ready], refs[ready + unread :]
    side = lax.rem(lax.axis_index("head"), 2)
    at_pos = block_starts(blocks, first_block, kv_refs[0].shape[2] // heads)
    dim = far_ref.shape[2]
    q_rows = steps * heads * group
    rows = steps * group
    slots = [(ref, side, n) for ref in near_refs for n in range(per)]
    slots += [(far_ref, j, n) for j in range(near) for n in range(per)]
    every = pl.ds(0, len(slots) * rows)
    each = q_rows + 2 * heads * steps
    at_limit = nreq * per * each + index * per
    lane = lax.broadcasted_iota(jnp.int32, (1, len(slots) * rows), 1)
    limit = jnp.zeros(lane.shape, F32)
    for i, (ref, lead, n) in enumerate(slots):
        wide = jnp.broadcast_to(ref[lead, at_limit + n : at_limit + n + 1, 0:1], lane.shape)
        limit = jnp.where(lane // rows == i, wide, limit)
    limit = limit.astype(jnp.int32)
    if finish:
        for i in range(ready):
            first = i // 2
            outs[i % 2][:, first : first + 1] = ready_refs[i][...]
    for head in range(heads):
        own = slice(head * group, (head + 1) * group)
        q = jnp.concatenate(
            [
                ref[lead, (index * per + n) * each : (index * per + n) * each + q_rows].reshape(steps, heads * group, dim)[:, own].reshape(rows, dim)
                for ref, lead, n in slots
            ],
            axis=0,
        )
        q6 = query_terms(q * scale)
        state = get_state(*state_in, head, every) if started else None
        for g, group_blocks in enumerate(in_pairs(list(range(blocks)))):
            parts = [
                score_block(key_terms(cache_head(kv_refs[b], 0, head, heads)), q6, limit, at_pos[b])
                for b in group_blocks
            ]
            vals = [value_terms(cache_head(kv_refs[b], 1, head, heads)) for b in group_blocks]
            if g == 0 and not started:
                drafts = [
                    jnp.concatenate(
                        [
                            ref[lead, pl.ds((index * per + n) * each + q_rows + which * heads + head, steps, stride=2 * heads), :]
                            for ref, lead, n in slots
                        ],
                        axis=0,
                    )
                    for which in range(2)
                ]
                s = lax.dot_general(
                    key_terms(drafts[0]), q6, (((1,), (1,)), ((), ())), preferred_element_type=F32
                )
                key = lax.broadcasted_iota(jnp.int32, s.shape, 0)
                row = lax.broadcasted_iota(jnp.int32, s.shape, 1)
                seen = (row // rows == key // steps) & (key % steps <= row % rows // group)
                parts.append(jnp.where(seen, s, NEG_FILL))
                vals.append(value_terms(drafts[1]))
            state = fold(state, parts, vals)
        if not finish:
            put_state(state, outs[0], outs[1], head, every)
            continue
        out = (state[2] * (1.0 / state[1])).T
        for i in range(len(slots)):
            dst, j, n = outs[i // (near * per)], i // per % near, i % per
            for step in range(steps):
                first = step * heads * group + head * group
                at = i * rows + step * group
                dst[j, dst.shape[1] - 1, n, first : first + group] = out[at : at + group]


def decode_request(
    index, sizes, near, far, kv_list, first_block, heads, group, steps, scale, state=None, finish=True, ready=(), after=()
):
    nreq, per = sizes
    count, packet_rows, dim = far.shape
    blocks = len(kv_list)
    q_rows = steps * heads * group
    all_rows = 2 * count * per * steps * group
    started = state is not None
    state = list(state) if started else []
    ready_flat = [a for one in ready for a in one]
    if finish:
        out_shape = [jax.ShapeDtypeStruct((count, len(ready) + 1, per, q_rows, dim), F32)] * 2
    else:
        out_shape = state_shapes(heads, dim, all_rows)
    keys = sum(kv.shape[2] for kv in kv_list) // heads
    plan = (index, nreq, per, count, blocks, first_block, started, finish, len(ready_flat), len(after))
    operands = count + 1 + blocks + len(state) + len(ready_flat)
    return pl.pallas_call(
        functools.partial(decode_kernel, plan, heads, group, steps, scale),
        in_specs=[VMEM_SPEC] * operands + [ANY_SPEC] * len(after),
        out_specs=[VMEM_SPEC] * len(out_shape),
        out_shape=out_shape,
        compiler_params=pltpu.CompilerParams(vmem_limit_bytes=12 * 2**20),
        cost_estimate=pl.CostEstimate(
            flops=all_rows * heads * keys * dim,
            bytes_accessed=4 * (4 * count * packet_rows * dim + 2 * heads * keys * dim),
            transcendentals=all_rows * heads * keys,
        ),
        name="decode",
    )(*near, far, *kv_list, *state, *ready_flat, *after)


def take_kernel(index, src, dst, sem):
    copy = pltpu.make_async_copy(src.at[pl.ds(index, 1)], dst, sem)
    copy.start()
    copy.wait()


def take(index, array):
    return pl.pallas_call(
        functools.partial(take_kernel, index),
        in_specs=[pl.BlockSpec(memory_space=pltpu.HBM)],
        out_specs=VMEM_SPEC,
        out_shape=jax.ShapeDtypeStruct((1,) + array.shape[1:], array.dtype),
        scratch_shapes=[pltpu.SemaphoreType.DMA],
        compiler_params=pltpu.CompilerParams(vmem_limit_bytes=4 * 2**20),
        name="take",
    )(array)


def pack_kernel(nreq, unread, lengths, q_ref, kv_ref, *refs):
    outs = refs[unread:]
    half = len(outs)
    per, q_rows, dim = q_ref.shape[1:]
    kv_rows = kv_ref.shape[2]
    rows = q_rows + kv_rows
    for j, out in enumerate(outs):
        pair = pair_of(lax.axis_index("head"), lax.axis_index("rep"), j, half)
        for c in range(2):
            tail = nreq * per * rows
            out[c, tail:] = jnp.zeros((out.shape[1] - tail, dim), F32)
            for i in range(nreq):
                request = (pair * 2 + c) * nreq + i
                for n in range(per):
                    at = i * per + n
                    out[c, at * rows : at * rows + q_rows] = q_ref[request, n]
                    out[c, at * rows + q_rows : (at + 1) * rows] = kv_ref[request, n]
                    reads = jnp.full((1, dim), lengths[request, n], jnp.int32)
                    out[c, tail + at : tail + at + 1] = reads.astype(F32)


def pack(lengths, q, kv, half, nreq, after):
    requests, per, q_rows, dim = q.shape
    each = nreq * per
    shape = jax.ShapeDtypeStruct((2, each * (q_rows + kv.shape[2]) + -(-each // 8) * 8, dim), F32)
    return pl.pallas_call(
        functools.partial(pack_kernel, nreq, len(after)),
        in_specs=[SMEM_SPEC, VMEM_SPEC, VMEM_SPEC] + [ANY_SPEC] * len(after),
        out_specs=[VMEM_SPEC] * half,
        out_shape=[shape] * half,
        compiler_params=pltpu.CompilerParams(vmem_limit_bytes=4 * 2**20),
        cost_estimate=pl.CostEstimate(flops=10**11, bytes_accessed=10**6, transcendentals=0),
        name="pack",
    )(lengths, q, kv, *after)


def other_kernel(count, *refs):
    out = refs[-1]
    for j, ref in enumerate(refs[:count]):
        out[j] = ref[1 - lax.rem(lax.axis_index("head"), 2)]


def other_side(near, after):
    return pl.pallas_call(
        functools.partial(other_kernel, len(near)),
        in_specs=[VMEM_SPEC] * len(near) + [ANY_SPEC] * len(after),
        out_specs=VMEM_SPEC,
        out_shape=jax.ShapeDtypeStruct((len(near),) + near[0].shape[1:], F32),
        compiler_params=pltpu.CompilerParams(vmem_limit_bytes=4 * 2**20),
        name="other_side",
    )(*near, *after)


def join_kernel(kept, back, *outs):
    side = lax.rem(lax.axis_index("head"), 2)
    for j, out in enumerate(outs):
        out[side] = kept[j]
        out[1 - side] = back[j]


def join(kept, back):
    count = kept.shape[0]
    return pl.pallas_call(
        join_kernel,
        in_specs=[VMEM_SPEC] * 2,
        out_specs=[VMEM_SPEC] * count,
        out_shape=[jax.ShapeDtypeStruct((2,) + kept.shape[1:], F32)] * count,
        compiler_params=pltpu.CompilerParams(vmem_limit_bytes=4 * 2**20),
        name="join",
    )(kept, back)


def place_kernel(*refs):
    o_ref, count = refs[-1], len(refs) - 1
    size = refs[0].shape[0]
    for j in range(count):
        o_ref[pl.ds(pair_of(lax.axis_index("head"), lax.axis_index("rep"), j, count) * size, size)] = refs[j][...]


def place(pieces):
    size, per, rows, dim = pieces[0].shape
    count = len(pieces)
    return pl.pallas_call(
        place_kernel,
        in_specs=[VMEM_SPEC] * count,
        out_specs=VMEM_SPEC,
        out_shape=jax.ShapeDtypeStruct((count * size, per, rows, dim), F32),
        compiler_params=pltpu.CompilerParams(vmem_limit_bytes=4 * 2**20),
        name="place",
    )(*pieces)


def on_device(kv_cache, prefill_q, decode_q, decode_kv, lengths, row_length):
    ctx_count, head_count, rep_count = lax.axis_size("ctx"), lax.axis_size("head"), lax.axis_size("rep")
    nreq, _, block_len, heads, dim = kv_cache.shape
    group = prefill_q.shape[2] // heads
    requests, per, steps, q_heads, _ = decode_q.shape
    scale = LOG2E / math.sqrt(dim)
    half = head_count // 2

    flat = kv_cache.reshape(nreq, 2, block_len * heads, dim)
    own = [take(i, flat) for i in range(nreq)]
    held = [[own[i]] for i in range(nreq)]
    for shift in range(1, ctx_count):
        perm = [((i + shift) % ctx_count, i) for i in range(ctx_count)]
        for i in range(nreq):
            held[i].append(lax.ppermute(own[i], "ctx", perm))

    routes = [
        [
            (s * rep_count + t, (pair_of(s, t, j, half) * 2 + core_of(t)) * rep_count + s)
            for s in range(head_count)
            for t in range(rep_count)
        ]
        for j in range(half)
    ]
    swap = [(i, i ^ 1) for i in range(head_count)]
    packets = pack(
        row_length,
        decode_q.reshape(requests, per, steps * q_heads, dim),
        decode_kv.reshape(requests, per, steps * 2 * heads, dim),
        half,
        nreq,
        own,
    )
    near = [lax.ppermute(packets[j], ("head", "rep"), routes[j]) for j in range(half)]
    last = nreq - 1
    prefill_state = prefill_request(last, lengths, prefill_q, held[last][:1], 0, heads, scale, finish=False, after=packets[:1])
    prefill_out, token = None, prefill_state[1]
    early = []
    for i in range(last):
        early.append(prefill_request(i, lengths, prefill_q, held[i][:1], 0, heads, scale, finish=False, after=(token,)))
        token = early[i][1]
    for i in range(last):
        prefill_out, token = prefill_request(
            i, lengths, prefill_q, held[i][1:], 1, heads, scale, state=early[i], carried=prefill_out, after=(token,)
        )
    far = lax.ppermute(other_side(near, (token,)), "head", swap)
    ready = [decode_request(i, (nreq, per), near, far, held[i], 0, heads, group, steps, scale) for i in range(last)]
    decode_state = decode_request(
        last, (nreq, per), near, far, held[last][:1], 0, heads, group, steps, scale, finish=False, after=ready[-1][:1]
    )
    kept, sent = decode_request(
        last, (nreq, per), near, far, held[last][1:], 1, heads, group, steps, scale, state=decode_state, ready=ready
    )
    prefill_out, _ = prefill_request(
        last, lengths, prefill_q, held[last][1:], 1, heads, scale, state=prefill_state, carried=prefill_out
    )
    joined = join(kept, lax.ppermute(sent, "head", swap))
    homes = [lax.ppermute(joined[j], ("head", "rep"), [(b, a) for a, b in routes[j]]) for j in range(half)]
    decode_out = place([a.reshape((2 * nreq,) + a.shape[2:]) for a in homes]).reshape(decode_q.shape)
    return (prefill_out, decode_out)


def solution(mesh):
    in_specs = (
        P("head", None, "ctx", "rep", None),
        P("head", "ctx", "rep", None),
        P(None, ("ctx", "rep"), None, "head", None),
        P(None, ("ctx", "rep"), None, None, "head", None),
        P(),
        P(None, ("ctx", "rep")),
    )
    out_specs = (P("head", "ctx", "rep", None), P(None, ("ctx", "rep"), None, "head", None))
    return jax.shard_map(on_device, mesh=mesh, in_specs=in_specs, out_specs=out_specs, check_vma=False)
```

```python
import functools
import math

import jax
import jax.numpy as jnp
from jax import lax
from jax.experimental import pallas as pl
from jax.experimental.pallas import tpu as pltpu
from jax.sharding import PartitionSpec as P

NEG_FILL = -1e30
LOG2E = math.log2(math.e)
F32 = jnp.float32
BF16 = jnp.bfloat16


def split_two(x):
    high = x.astype(BF16)
    return high, (x - high.astype(F32)).astype(BF16)


def split_three(x):
    high = x.astype(BF16)
    rest = x - high.astype(F32)
    mid = rest.astype(BF16)
    return high, mid, (rest - mid.astype(F32)).astype(BF16)


def query_terms(q):
    a, b, c = split_three(q)
    return jnp.concatenate([a, b, a, b, a, c], axis=-1)


def key_terms(k):
    a, b, c = split_three(k)
    return jnp.concatenate([a, a, b, b, c, a], axis=-1)


def value_terms(v):
    return jnp.concatenate(split_two(v.T), axis=0)


def score_block(k6, q6, limit, first_pos):
    s = lax.dot_general(k6, q6, (((1,), (1,)), ((), ())), preferred_element_type=F32)
    return jnp.where(lax.broadcasted_iota(jnp.int32, s.shape, 0) < limit - first_pos, s, NEG_FILL)


def weighted(vv, p):
    dim = vv.shape[0] // 2
    a, b = split_two(p)
    both = jnp.dot(vv, a, preferred_element_type=F32)
    return (both[:dim] + both[dim:]) + jnp.dot(vv[:dim], b, preferred_element_type=F32)


def fold(state, scores, values):
    top = functools.reduce(jnp.maximum, [jnp.max(s, axis=0, keepdims=True) for s in scores])
    if state is not None:
        top = jnp.maximum(top, state[0])
    weights = [jnp.exp2(s - top) for s in scores]
    total = functools.reduce(jnp.add, [jnp.sum(w, axis=0, keepdims=True) for w in weights])
    acc = functools.reduce(jnp.add, [weighted(vv, w) for vv, w in zip(values, weights)])
    if state is not None:
        factor = jnp.exp2(state[0] - top)
        total = total + state[1] * factor
        acc = acc + state[2] * factor
    return top, total, acc


def in_pairs(blocks):
    return [blocks[i : i + 2] for i in range(0, len(blocks), 2)]


def cache_head(ref, which, head, heads):
    return ref[0, which, pl.ds(head, ref.shape[2] // heads, stride=heads), :]


def put_state(state, acc_ref, stat_ref, head, cols):
    acc_ref[head, :, cols] = state[2]
    stat_ref[head, 0:1, cols] = state[0]
    stat_ref[head, 1:2, cols] = state[1]


def get_state(acc_ref, stat_ref, head, cols):
    return stat_ref[head, 0:1, cols], stat_ref[head, 1:2, cols], acc_ref[head, :, cols]


def state_shapes(heads, dim, rows):
    return [jax.ShapeDtypeStruct((heads, dim, rows), F32), jax.ShapeDtypeStruct((heads, 8, rows), F32)]


def pair_of(s, t, j, half):
    return (t // 2 + j + 1 + core_of(t) + s // half + s % 2) % half


def core_of(t):
    return (t + t // 2) % 2


def block_starts(count, first, block_len):
    here, total = lax.axis_index("ctx"), lax.axis_size("ctx")
    return [lax.rem(here + (first + b), total) * block_len for b in range(count)]


def prefill_kernel(plan, heads, scale, lengths, q_ref, *refs):
    index, blocks, first_block, started, finish, unread = plan
    kv_refs, refs = refs[:blocks], refs[blocks:]
    state_in = refs[:2] if started else None
    outs = refs[(2 if started else 0) + unread :]
    _, span, q_heads, dim = q_ref.shape
    group = q_heads // heads
    chunk = min(span, CHUNK)
    total = lax.axis_size("ctx") * span
    begin = lengths[lax.axis_index("head") * q_ref.shape[0] + index] - total + lax.axis_index("ctx") * span
    at_pos = block_starts(blocks, first_block, kv_refs[0].shape[2] // heads)
    keys = [[key_terms(cache_head(ref, 0, h, heads)) for ref in kv_refs] for h in range(heads)]
    vals = [[value_terms(cache_head(ref, 1, h, heads)) for ref in kv_refs] for h in range(heads)]
    items = [(first, h) for first in range(0, span, chunk) for h in range(heads)]
    groups = in_pairs(list(range(blocks)))

    def scores(item):
        first, h = item
        q = q_ref[index, first : first + chunk, h * group : (h + 1) * group].reshape(chunk * group, dim) * scale
        q6 = query_terms(q)
        limit = begin + first + 1 + lax.broadcasted_iota(jnp.int32, (1, chunk * group), 1) // group
        return [
            functools.partial(
                lambda g: [score_block(keys[h][b], q6, limit, at_pos[b]) for b in g], g
            )
            for g in groups
        ]

    steps = [(n, g, make) for n, item in enumerate(items) for g, make in zip(groups, scores(item))]
    ahead = steps[0][2]()
    state = None
    copies = []
    for at, (n, g, _) in enumerate(steps):
        now, ahead = ahead, steps[at + 1][2]() if at + 1 < len(steps) else None
        first, h = items[n]
        cols = pl.ds(first * group, chunk * group)
        if g is groups[0]:
            state = get_state(*state_in, h, cols) if started else None
        state = fold(state, now, [vals[h][b] for b in g])
        if g is not groups[-1]:
            continue
        if not finish:
            put_state(state, outs[0], outs[1], h, cols)
            continue
        out_ref, hold, sems = outs[0], outs[-2], outs[-1]
        hold[n] = (state[2] * (1.0 / state[1])).T.reshape(chunk, group, dim)
        copy = pltpu.make_async_copy(
            hold.at[n], out_ref.at[index, pl.ds(first, chunk), pl.ds(h * group, group)], sems.at[n]
        )
        copy.start()
        copies.append(copy)
    if finish:
        outs[1][...] = jnp.zeros_like(outs[1])
    for copy in copies:
        copy.wait()


CHUNK = 128
SMEM_SPEC = pl.BlockSpec(memory_space=pltpu.SMEM)
VMEM_SPEC = pl.BlockSpec(memory_space=pltpu.VMEM)
ANY_SPEC = pl.BlockSpec(memory_space=pl.ANY)


def prefill_request(index, lengths, prefill_q, kv_list, first_block, heads, scale, state=None, finish=True, carried=None, after=()):
    nreq, span, q_heads, dim = prefill_q.shape
    group = q_heads // heads
    blocks = len(kv_list)
    started = state is not None
    state = list(state) if started else []
    unread = list(after) + ([carried] if carried is not None else [])
    alias = {2 + blocks + len(state) + len(after): 0} if carried is not None else {}
    keys = sum(kv.shape[2] for kv in kv_list) // heads
    scratch = []
    if finish:
        out_specs = [ANY_SPEC, VMEM_SPEC]
        out_shape = [jax.ShapeDtypeStruct(prefill_q.shape, F32), jax.ShapeDtypeStruct((8, 128), F32)]
        chunk = min(span, CHUNK)
        items = span // chunk * heads
        scratch = [pltpu.VMEM((items, chunk, group, dim), F32), pltpu.SemaphoreType.DMA((items,))]
    else:
        out_specs = [VMEM_SPEC, VMEM_SPEC]
        out_shape = state_shapes(heads, dim, span * group)
    return pl.pallas_call(
        functools.partial(prefill_kernel, (index, blocks, first_block, started, finish, len(unread)), heads, scale),
        in_specs=[SMEM_SPEC] + [VMEM_SPEC] * (1 + blocks + len(state)) + [ANY_SPEC] * len(unread),
        out_specs=out_specs,
        out_shape=out_shape,
        scratch_shapes=scratch,
        input_output_aliases=alias,
        compiler_params=pltpu.CompilerParams(vmem_limit_bytes=16 * 2**20),
        cost_estimate=pl.CostEstimate(
            flops=span * q_heads * keys * dim,
            bytes_accessed=4 * (2 * span * q_heads * dim + 2 * heads * keys * dim),
            transcendentals=span * q_heads * keys,
        ),
        name="prefill",
    )(lengths, prefill_q, *kv_list, *state, *unread)


def decode_kernel(plan, heads, group, steps, scale, *refs):
    index, nreq, per, near, blocks, first_block, started, finish, ready, unread = plan
    near_refs, far_ref, refs = refs[:near], refs[near], refs[near + 1 :]
    kv_refs, refs = refs[:blocks], refs[blocks:]
    state_in = refs[:2] if started else None
    refs = refs[2 if started else 0 :]
    ready_refs, outs = refs[:ready], refs[ready + unread :]
    side = lax.rem(lax.axis_index("head"), 2)
    at_pos = block_starts(blocks, first_block, kv_refs[0].shape[2] // heads)
    dim = far_ref.shape[2]
    q_rows = steps * heads * group
    rows = steps * group
    slots = [(ref, side, n) for ref in near_refs for n in range(per)]
    slots += [(far_ref, j, n) for j in range(near) for n in range(per)]
    every = pl.ds(0, len(slots) * rows)
    each = q_rows + 2 * heads * steps
    at_limit = nreq * per * each + index * per
    lane = lax.broadcasted_iota(jnp.int32, (1, len(slots) * rows), 1)
    limit = jnp.zeros(lane.shape, F32)
    for i, (ref, lead, n) in enumerate(slots):
        wide = jnp.broadcast_to(ref[lead, at_limit + n : at_limit + n + 1, 0:1], lane.shape)
        limit = jnp.where(lane // rows == i, wide, limit)
    limit = limit.astype(jnp.int32)
    if finish:
        for i in range(ready):
            first = i // 2
            outs[i % 2][:, first : first + 1] = ready_refs[i][...]
    for head in range(heads):
        own = slice(head * group, (head + 1) * group)
        q = jnp.concatenate(
            [
                ref[lead, (index * per + n) * each : (index * per + n) * each + q_rows].reshape(steps, heads * group, dim)[:, own].reshape(rows, dim)
                for ref, lead, n in slots
            ],
            axis=0,
        )
        q6 = query_terms(q * scale)
        state = get_state(*state_in, head, every) if started else None
        for g, group_blocks in enumerate(in_pairs(list(range(blocks)))):
            parts = [
                score_block(key_terms(cache_head(kv_refs[b], 0, head, heads)), q6, limit, at_pos[b])
                for b in group_blocks
            ]
            vals = [value_terms(cache_head(kv_refs[b], 1, head, heads)) for b in group_blocks]
            if g == 0 and not started:
                drafts = [
                    jnp.concatenate(
                        [
                            ref[lead, pl.ds((index * per + n) * each + q_rows + which * heads + head, steps, stride=2 * heads), :]
                            for ref, lead, n in slots
                        ],
                        axis=0,
                    )
                    for which in range(2)
                ]
                s = lax.dot_general(
                    key_terms(drafts[0]), q6, (((1,), (1,)), ((), ())), preferred_element_type=F32
                )
                key = lax.broadcasted_iota(jnp.int32, s.shape, 0)
                row = lax.broadcasted_iota(jnp.int32, s.shape, 1)
                seen = (row // rows == key // steps) & (key % steps <= row % rows // group)
                parts.append(jnp.where(seen, s, NEG_FILL))
                vals.append(value_terms(drafts[1]))
            state = fold(state, parts, vals)
        if not finish:
            put_state(state, outs[0], outs[1], head, every)
            continue
        out = (state[2] * (1.0 / state[1])).T
        for i in range(len(slots)):
            dst, j, n = outs[i // (near * per)], i // per % near, i % per
            for step in range(steps):
                first = step * heads * group + head * group
                at = i * rows + step * group
                dst[j, dst.shape[1] - 1, n, first : first + group] = out[at : at + group]


def decode_request(
    index, sizes, near, far, kv_list, first_block, heads, group, steps, scale, state=None, finish=True, ready=(), after=()
):
    nreq, per = sizes
    count, packet_rows, dim = far.shape
    blocks = len(kv_list)
    q_rows = steps * heads * group
    all_rows = 2 * count * per * steps * group
    started = state is not None
    state = list(state) if started else []
    ready_flat = [a for one in ready for a in one]
    if finish:
        out_shape = [jax.ShapeDtypeStruct((count, len(ready) + 1, per, q_rows, dim), F32)] * 2
    else:
        out_shape = state_shapes(heads, dim, all_rows)
    keys = sum(kv.shape[2] for kv in kv_list) // heads
    plan = (index, nreq, per, count, blocks, first_block, started, finish, len(ready_flat), len(after))
    operands = count + 1 + blocks + len(state) + len(ready_flat)
    return pl.pallas_call(
        functools.partial(decode_kernel, plan, heads, group, steps, scale),
        in_specs=[VMEM_SPEC] * operands + [ANY_SPEC] * len(after),
        out_specs=[VMEM_SPEC] * len(out_shape),
        out_shape=out_shape,
        compiler_params=pltpu.CompilerParams(vmem_limit_bytes=12 * 2**20),
        cost_estimate=pl.CostEstimate(
            flops=all_rows * heads * keys * dim,
            bytes_accessed=4 * (4 * count * packet_rows * dim + 2 * heads * keys * dim),
            transcendentals=all_rows * heads * keys,
        ),
        name="decode",
    )(*near, far, *kv_list, *state, *ready_flat, *after)


def take_kernel(index, src, dst, sem):
    copy = pltpu.make_async_copy(src.at[pl.ds(index, 1)], dst, sem)
    copy.start()
    copy.wait()


def take(index, array):
    return pl.pallas_call(
        functools.partial(take_kernel, index),
        in_specs=[pl.BlockSpec(memory_space=pltpu.HBM)],
        out_specs=VMEM_SPEC,
        out_shape=jax.ShapeDtypeStruct((1,) + array.shape[1:], array.dtype),
        scratch_shapes=[pltpu.SemaphoreType.DMA],
        compiler_params=pltpu.CompilerParams(vmem_limit_bytes=4 * 2**20),
        name="take",
    )(array)


def pack_kernel(nreq, unread, lengths, q_ref, kv_ref, *refs):
    outs = refs[unread:]
    half = len(outs)
    per, q_rows, dim = q_ref.shape[1:]
    kv_rows = kv_ref.shape[2]
    rows = q_rows + kv_rows
    for j, out in enumerate(outs):
        pair = pair_of(lax.axis_index("head"), lax.axis_index("rep"), j, half)
        for c in range(2):
            tail = nreq * per * rows
            out[c, tail:] = jnp.zeros((out.shape[1] - tail, dim), F32)
            for i in range(nreq):
                request = (pair * 2 + c) * nreq + i
                for n in range(per):
                    at = i * per + n
                    out[c, at * rows : at * rows + q_rows] = q_ref[request, n]
                    out[c, at * rows + q_rows : (at + 1) * rows] = kv_ref[request, n]
                    reads = jnp.full((1, dim), lengths[request, n], jnp.int32)
                    out[c, tail + at : tail + at + 1] = reads.astype(F32)


def pack(lengths, q, kv, half, nreq, after):
    requests, per, q_rows, dim = q.shape
    each = nreq * per
    shape = jax.ShapeDtypeStruct((2, each * (q_rows + kv.shape[2]) + -(-each // 8) * 8, dim), F32)
    return pl.pallas_call(
        functools.partial(pack_kernel, nreq, len(after)),
        in_specs=[SMEM_SPEC, VMEM_SPEC, VMEM_SPEC] + [ANY_SPEC] * len(after),
        out_specs=[VMEM_SPEC] * half,
        out_shape=[shape] * half,
        compiler_params=pltpu.CompilerParams(vmem_limit_bytes=4 * 2**20),
        cost_estimate=pl.CostEstimate(flops=10**11, bytes_accessed=10**6, transcendentals=0),
        name="pack",
    )(lengths, q, kv, *after)


def other_kernel(count, *refs):
    out = refs[-1]
    for j, ref in enumerate(refs[:count]):
        out[j] = ref[1 - lax.rem(lax.axis_index("head"), 2)]


def other_side(near, after):
    return pl.pallas_call(
        functools.partial(other_kernel, len(near)),
        in_specs=[VMEM_SPEC] * len(near) + [ANY_SPEC] * len(after),
        out_specs=VMEM_SPEC,
        out_shape=jax.ShapeDtypeStruct((len(near),) + near[0].shape[1:], F32),
        compiler_params=pltpu.CompilerParams(vmem_limit_bytes=4 * 2**20),
        name="other_side",
    )(*near, *after)


def join_kernel(kept, back, *outs):
    side = lax.rem(lax.axis_index("head"), 2)
    for j, out in enumerate(outs):
        out[side] = kept[j]
        out[1 - side] = back[j]


def join(kept, back):
    count = kept.shape[0]
    return pl.pallas_call(
        join_kernel,
        in_specs=[VMEM_SPEC] * 2,
        out_specs=[VMEM_SPEC] * count,
        out_shape=[jax.ShapeDtypeStruct((2,) + kept.shape[1:], F32)] * count,
        compiler_params=pltpu.CompilerParams(vmem_limit_bytes=4 * 2**20),
        name="join",
    )(kept, back)


def place_kernel(*refs):
    refs, o_ref, sems = refs[:-2], refs[-2], refs[-1]
    count = len(refs)
    size = refs[0].shape[0]
    copies = []
    for j in range(count):
        pair = pair_of(lax.axis_index("head"), lax.axis_index("rep"), j, count)
        copies.append(pltpu.make_async_copy(refs[j], o_ref.at[pl.ds(pair * size, size)], sems.at[j]))
        copies[-1].start()
    for copy in copies:
        copy.wait()


def place(pieces):
    size, per, rows, dim = pieces[0].shape
    count = len(pieces)
    return pl.pallas_call(
        place_kernel,
        in_specs=[VMEM_SPEC] * count,
        out_specs=ANY_SPEC,
        out_shape=jax.ShapeDtypeStruct((count * size, per, rows, dim), F32),
        scratch_shapes=[pltpu.SemaphoreType.DMA((count,))],
        compiler_params=pltpu.CompilerParams(vmem_limit_bytes=4 * 2**20),
        name="place",
    )(*pieces)


def on_device(kv_cache, prefill_q, decode_q, decode_kv, lengths, row_length):
    ctx_count, head_count, rep_count = lax.axis_size("ctx"), lax.axis_size("head"), lax.axis_size("rep")
    nreq, _, block_len, heads, dim = kv_cache.shape
    group = prefill_q.shape[2] // heads
    requests, per, steps, q_heads, _ = decode_q.shape
    scale = LOG2E / math.sqrt(dim)
    half = head_count // 2

    flat = kv_cache.reshape(nreq, 2, block_len * heads, dim)
    own = [take(i, flat) for i in range(nreq)]
    held = [[own[i]] for i in range(nreq)]
    for shift in range(1, ctx_count):
        perm = [((i + shift) % ctx_count, i) for i in range(ctx_count)]
        for i in range(nreq):
            held[i].append(lax.ppermute(own[i], "ctx", perm))

    routes = [
        [
            (s * rep_count + t, (pair_of(s, t, j, half) * 2 + core_of(t)) * rep_count + s)
            for s in range(head_count)
            for t in range(rep_count)
        ]
        for j in range(half)
    ]
    swap = [(i, i ^ 1) for i in range(head_count)]
    packets = pack(
        row_length,
        decode_q.reshape(requests, per, steps * q_heads, dim),
        decode_kv.reshape(requests, per, steps * 2 * heads, dim),
        half,
        nreq,
        own,
    )
    near = [lax.ppermute(packets[j], ("head", "rep"), routes[j]) for j in range(half)]
    last = nreq - 1
    prefill_state = prefill_request(last, lengths, prefill_q, held[last][:1], 0, heads, scale, finish=False, after=packets[:1])
    prefill_out, token = None, prefill_state[1]
    early = []
    for i in range(last):
        early.append(prefill_request(i, lengths, prefill_q, held[i][:1], 0, heads, scale, finish=False, after=(token,)))
        token = early[i][1]
    for i in range(last):
        prefill_out, token = prefill_request(
            i, lengths, prefill_q, held[i][1:], 1, heads, scale, state=early[i], carried=prefill_out, after=(token,)
        )
    far = lax.ppermute(other_side(near, (token,)), "head", swap)
    ready = [decode_request(i, (nreq, per), near, far, held[i], 0, heads, group, steps, scale) for i in range(last)]
    decode_state = decode_request(
        last, (nreq, per), near, far, held[last][:1], 0, heads, group, steps, scale, finish=False, after=ready[-1][:1]
    )
    kept, sent = decode_request(
        last, (nreq, per), near, far, held[last][1:], 1, heads, group, steps, scale, state=decode_state, ready=ready
    )
    prefill_out, _ = prefill_request(
        last, lengths, prefill_q, held[last][1:], 1, heads, scale, state=prefill_state, carried=prefill_out
    )
    joined = join(kept, lax.ppermute(sent, "head", swap))
    homes = [lax.ppermute(joined[j], ("head", "rep"), [(b, a) for a, b in routes[j]]) for j in range(half)]
    decode_out = place([a.reshape((2 * nreq,) + a.shape[2:]) for a in homes]).reshape(decode_q.shape)
    return (prefill_out, decode_out)


def solution(mesh):
    in_specs = (
        P("head", None, "ctx", "rep", None),
        P("head", "ctx", "rep", None),
        P(None, ("ctx", "rep"), None, "head", None),
        P(None, ("ctx", "rep"), None, None, "head", None),
        P(),
        P(None, ("ctx", "rep")),
    )
    out_specs = (P("head", "ctx", "rep", None), P(None, ("ctx", "rep"), None, "head", None))
    return jax.shard_map(on_device, mesh=mesh, in_specs=in_specs, out_specs=out_specs, check_vma=False)
```
